32 devices in a mesh: rep: 8 (over y, x, core), sp: 4 (over z).
Axes of the slice: x: 2, y: 2, z: 4, core: 2. Of those that a mesh axis runs over, the one named last changes fastest.
Arguments:
- positions: float32 [8, 3, 32768], P('rep', None, 'sp'), may hold values from -18 to 18
- velocities: float32 [8, 3, 32768], P('rep', None, 'sp'), may hold values from -6 to 6
- strength: float32 [8, 32768], P('rep', 'sp'), may hold values from 0.5 to 2
- inv_mass: float32 [8, 32768], P('rep', 'sp'), may hold values from 0.1 to 1
- tile_lists: int32 [8, 4, 256, 4], P('rep', None, 'sp'), may hold values from 0 to 127, as said below
- solute_index: int32 [8, 1024], P('rep', 'sp'), may hold values from 0 to 8191, as said below
- scatter_weight: float32 [8, 1024], P('rep', 'sp'), may hold values from 0.3 to 3
- intensity_exp: float32 [48], replicated, may hold values from 0.5 to 3
- precision: float32 [48], replicated, may hold values from 1 to 4
Outputs:
- positions_out: float32 [8, 3, 32768], P('rep', None, 'sp')
- velocities_out: float32 [8, 3, 32768], P('rep', None, 'sp')
The draws below stay inside these ranges and needn't reach their ends.
Inputs may be any that keep to these rules, and one draw needn't show every extreme that they name: `tile_lists`: for each replica, step and local block b of a domain (numbered 0 to 63), the 4 entries are distinct extended block numbers from b to b + 64, among them b, b + 32 and b + 64. `solute_index`: within each replica and domain the 256 entries are distinct local atom numbers.
All inputs are finite; a program needn't handle non-finite values.
Results may differ from the reference program's by a relative error of at most 0.0001.
Values sent between devices are 32-bit elements; how exact they have to be, the bound alone decides.
A program may use at most 128 MiB of HBM per device.

```python
import math
import jax
import jax.numpy as jnp
from jax import lax

ATOM_DEV = 8192
SOL_DEV = 256
NQ = 48
M = 784
K = 4
BLOCK = 128
OUTER = 2
INNER = 2
STEPS = 4
NB = 64
HB = 32
HALO = 4096
REPLICAS = 8
ATOMS = 32768
NBLK = 256
SOL_ALL = 1024


def draw_tile_lists(key, part):
    grid_shape = (REPLICAS, STEPS, NBLK)
    local_block = jnp.arange(NBLK, dtype=jnp.int32) % NB
    inner_count = 2 * HB - 2
    steps_below = jnp.arange(1, HB, dtype=jnp.int32)
    offsets = jnp.concatenate([-steps_below[::-1], steps_below])
    scores = jax.random.randint(key, grid_shape + (inner_count,), 0, 1 << 20) * inner_count + jnp.arange(inner_count, dtype=jnp.int32)
    ranked = jnp.argsort(scores, axis=-1, stable=True)[..., :K - 3]
    chosen = offsets[ranked]
    fixed_part = jnp.broadcast_to(jnp.array([0, -HB, HB], jnp.int32), grid_shape + (3,))
    entries = jnp.concatenate([fixed_part, chosen], axis=-1)
    return (entries + HB + local_block[None, None, :, None]).astype(jnp.int32)


def draw_solute_index(key, part):
    domains = SOL_ALL // SOL_DEV
    first_key = jax.random.fold_in(key, 11)
    second_key = jax.random.fold_in(key, 23)
    atom_ids = jnp.arange(ATOM_DEV, dtype=jnp.int32)
    scores = jax.random.randint(first_key, (REPLICAS, domains, ATOM_DEV), 0, 1 << 14) * ATOM_DEV + atom_ids
    scores = jnp.where(atom_ids == 0, -2, jnp.where(atom_ids == ATOM_DEV - 1, -1, scores))
    ranked = jnp.argsort(scores, axis=-1, stable=True)[..., :SOL_DEV].astype(jnp.int32)
    shuffle_scores = jax.random.randint(second_key, (REPLICAS, domains, SOL_DEV), 0, 1 << 14) * SOL_DEV + jnp.arange(SOL_DEV, dtype=jnp.int32)
    order_index = jnp.argsort(shuffle_scores, axis=-1, stable=True)
    picked = jnp.take_along_axis(ranked, order_index, axis=-1)
    return picked.reshape(REPLICAS, domains * SOL_DEV).astype(jnp.int32)


def level_of(stream_key, shape, shards, low, top_value):
    def one(dim, shards_of):
        steps = jax.random.uniform(jax.random.fold_in(jax.random.fold_in(stream_key, 6), dim), (shards_of,), jnp.float32, low / len(shards), top_value / len(shards))
        return jnp.repeat(jnp.exp(steps), shape[dim] // shards_of).reshape((-1,) + (1,) * (len(shape) - dim - 1))

    gain = one(*shards[0])
    for cut in shards[1:]:
        gain = gain * one(*cut)
    return gain


def bell_draw(key, dims, width, reach, shards=(), held_as=jnp.bfloat16):
    drawn = jax.random.normal(key, dims, jnp.float32) * width
    if len(shards) > 0:
        drawn = level_of(key, dims, shards, -0.22, 0.18) * drawn
    return jnp.clip(drawn, min=-reach, max=reach).astype(held_as)


def setup_inputs(seed: int = 0) -> dict:
    key_of = jax.random.split(jax.random.key(seed), 10)
    return {
        "positions": bell_draw(key_of[0], (REPLICAS, 3, ATOMS), 3.0, 18.0, ((0, 8), (2, 4)), jnp.float32),
        "velocities": bell_draw(key_of[1], (REPLICAS, 3, ATOMS), 1.0, 6.0, ((0, 8), (2, 4)), jnp.float32),
        "strength": jnp.clip(jnp.exp(math.log(2.0) - 1.3862944 * jax.random.uniform(key_of[2], (REPLICAS, ATOMS), jnp.float32) ** level_of(key_of[2], (REPLICAS, ATOMS), ((0, 8), (1, 4)), -0.2, 0.2)), 0.5, 2.0),
        "inv_mass": jnp.clip(jnp.exp(math.log(1.0) - 2.3025851 * jax.random.uniform(key_of[3], (REPLICAS, ATOMS), jnp.float32) ** level_of(key_of[3], (REPLICAS, ATOMS), ((0, 8), (1, 4)), -0.2, 0.2)), 0.1, 1.0),
        "tile_lists": draw_tile_lists(jax.random.fold_in(key_of[9], 71), 0),
        "solute_index": draw_solute_index(jax.random.fold_in(key_of[9], 71), 0),
        "scatter_weight": jnp.clip(jnp.exp(math.log(3.0) - 2.3025851 * jax.random.uniform(key_of[6], (REPLICAS, SOL_ALL), jnp.float32) ** level_of(key_of[6], (REPLICAS, SOL_ALL), ((0, 8), (1, 4)), -0.2, 0.2)), 0.3, 3.0),
        "intensity_exp": jnp.clip(jax.random.uniform(key_of[7], (NQ,), jnp.float32, 0.5, 3.0), 0.5, 3.0),
        "precision": jnp.clip(jnp.exp(jax.random.uniform(key_of[8], (NQ,), jnp.float32, math.log(1.0), math.log(4.0))), 1.0, 4.0),
    }


TIME_STEP = 0.05
PAIR_STRENGTH = 0.2
HALF_INVERSE = 0.03125
shell_batch = 8
group_limit = 8

def directions(total_terms):
    order_index = jnp.arange(total_terms, dtype=jnp.int32)
    height = 1.0 - (2.0 * order_index.astype(jnp.float32) + 1.0) / total_terms
    radius = jnp.sqrt(1.0 - height * height)
    azimuth = (order_index * 610 % 987).astype(jnp.float32) * (2.0 * math.pi / 987.0)
    return (radius * jnp.cos(azimuth), radius * jnp.sin(azimuth), height)

def shell_values(total_shells):
    return 1.0 + 3.0 * jnp.arange(total_shells, dtype=jnp.int32).astype(jnp.float32) / total_shells

def projection(points, dir_x, dir_y, dir_z):
    return dir_x[:, None] * points[0][None, :] + dir_y[:, None] * points[1][None, :] + dir_z[:, None] * points[2][None, :]

def amplitude_terms(project, weights, shell_q):
    shell_blocks = shell_q.reshape(-1, shell_batch)

    def one_block(shell_block):
        phases = shell_block[:, None, None] * project[None]
        return jnp.stack([lax.optimization_barrier(jnp.sum(weights * jnp.cos(phases), axis=-1)), lax.optimization_barrier(jnp.sum(weights * jnp.sin(phases), axis=-1))])
    result = lax.map(one_block, shell_blocks)
    return jnp.transpose(result, (1, 0, 2, 3)).reshape(2, -1, project.shape[0])

def shell_intensity(amplitude):
    return lax.optimization_barrier(jnp.mean(amplitude[0] * amplitude[0] + amplitude[1] * amplitude[1], axis=-1))

def scale_grad(amplitude, intensity, precision, intensity_exp, total_terms):
    coef_shell = 2.0 * precision * (intensity - intensity_exp) / total_terms
    return coef_shell[None, :, None] * amplitude

def restraint_forces(project, weights, shell_q, weight_grad, dir_x, dir_y, dir_z):
    shell_blocks = shell_q.reshape(-1, shell_batch)
    grad_real = weight_grad[0].reshape(-1, shell_batch, project.shape[0])
    grad_imag = weight_grad[1].reshape(-1, shell_batch, project.shape[0])

    def add_block(running, pieces):
        shell_block, block_real, block_imag = pieces
        phases = shell_block[:, None, None] * project[None]
        block_term = lax.optimization_barrier(jnp.sum(shell_block[:, None, None] * (block_imag[:, :, None] * jnp.cos(phases) - block_real[:, :, None] * jnp.sin(phases)), axis=0))
        return (running + block_term, None)
    running, unused = lax.scan(add_block, jnp.zeros(project.shape, jnp.float32), (shell_blocks, grad_real, grad_imag))
    return jnp.stack([-weights * lax.optimization_barrier(jnp.sum(dir_x[:, None] * running, axis=0)), -weights * lax.optimization_barrier(jnp.sum(dir_y[:, None] * running, axis=0)), -weights * lax.optimization_barrier(jnp.sum(dir_z[:, None] * running, axis=0))])

def pair_group(own_rows, near_rows, coupling):
    delta_list = [own_rows[component][:, :, None] - near_rows[component][:, None, :] for component in range(3)]
    distance = delta_list[0] * delta_list[0] + delta_list[1] * delta_list[1] + delta_list[2] * delta_list[2]
    pair_weight = coupling * own_rows[3][:, :, None] * near_rows[3][:, None, :] * jnp.exp(-HALF_INVERSE * distance)
    return jnp.stack([lax.optimization_barrier(jnp.sum(pair_weight * delta, axis=-1)) for delta in delta_list])

def pair_forces(own_blocks, ext_blocks, tile_list):
    block_count, neighbours = tile_list.shape
    block_width = own_blocks.shape[2]
    group_size = min(group_limit, block_count)
    coupling = PAIR_STRENGTH / math.sqrt(neighbours * block_width)
    nearby = jnp.take(ext_blocks, tile_list.reshape(-1), axis=1).reshape(4, block_count // group_size, group_size, neighbours * block_width)
    grouped = own_blocks.reshape(4, block_count // group_size, group_size, block_width)

    def one_group(pieces):
        return pair_group(pieces[0], pieces[1], coupling)
    result = lax.map(one_group, (jnp.moveaxis(grouped, 1, 0), jnp.moveaxis(nearby, 1, 0)))
    return jnp.moveaxis(result, 0, 1).reshape(3, -1)

def take_columns(row_set, chosen):
    return jnp.take(row_set, chosen, axis=1)

def take_entries(row_set, chosen):
    return jnp.take(row_set, chosen)

def add_columns(row_set, chosen, extra):
    return row_set.at[:, chosen].add(extra)

def reference(positions, velocities, strength, inv_mass, tile_lists, solute_index, scatter_weight, intensity_exp, precision):
    dir_x, dir_y, dir_z = directions(M)
    shell_q = shell_values(NQ)
    first_block = jnp.arange(NBLK, dtype=jnp.int32) // NB * NB
    atom_base = jnp.arange(SOL_ALL, dtype=jnp.int32) // SOL_DEV * ATOM_DEV
    atom_index = (solute_index + atom_base[None, :]).astype(jnp.int32)
    scale_norm = 1.0 / math.sqrt(SOL_ALL)
    coords_now = positions
    speed_now = velocities
    mass_here = jax.vmap(take_entries)(inv_mass, atom_index)
    for outer_step in range(OUTER):
        points = jax.vmap(take_columns)(coords_now, atom_index)

        def replica_terms(pieces):
            project = projection(pieces[0], dir_x, dir_y, dir_z)
            return amplitude_terms(project, pieces[1], shell_q) * scale_norm
        amplitude = lax.map(replica_terms, (points, scatter_weight))
        intensity = lax.optimization_barrier(jnp.mean(jax.vmap(shell_intensity)(amplitude), axis=0))

        def replica_kick(pieces):
            project = projection(pieces[0], dir_x, dir_y, dir_z)
            weight_grad = scale_grad(pieces[2], intensity, precision, intensity_exp, M)
            return restraint_forces(project, pieces[1], shell_q, weight_grad, dir_x, dir_y, dir_z)
        saxs_kick = lax.map(replica_kick, (points, scatter_weight, amplitude))
        for inner_step in range(INNER):
            tile_step = (tile_lists[:, outer_step * INNER + inner_step] + first_block[None, :, None]).astype(jnp.int32)

            def replica_pairs(pieces):
                coords_rep, charge_rep, tile_rep = pieces
                rows_all = jnp.concatenate([coords_rep, charge_rep[None, :]], axis=0)
                padded = jnp.pad(rows_all, ((0, 0), (HALO, HALO)))
                return pair_forces(rows_all.reshape(4, NBLK, BLOCK), padded.reshape(4, NBLK + 2 * HB, BLOCK), tile_rep)
            pair_push = lax.map(replica_pairs, (coords_now, strength, tile_step))
            speed_now = speed_now + TIME_STEP * inv_mass[:, None, :] * pair_push
            coords_now = coords_now + TIME_STEP * speed_now
        impulse = INNER * TIME_STEP * mass_here[:, None, :] * saxs_kick
        speed_now = jax.vmap(add_columns)(speed_now, atom_index, impulse)
    return (coords_now, speed_now)
```

```python
import functools
import math

import jax
import jax.numpy as jnp
import numpy as np
from jax import lax
from jax.experimental import pallas as pl
from jax.experimental.pallas import tpu as pltpu
from jax.sharding import PartitionSpec as P

M = 784
OUTER = 2
INNER = 2
TIME_STEP = 0.05
PAIR_STRENGTH = 0.2
HALF_INVERSE = 0.03125
LANES = 128
GROUP = 16
ROWS = 48
F32 = jnp.float32
BF16 = jnp.bfloat16
MESH = pl.DeviceIdType.MESH


def direction_table(shards):
    order = np.arange(M)
    height = 1.0 - (2.0 * order + 1.0) / M
    radius = np.sqrt(1.0 - height * height)
    azimuth = (order * 610 % 987) * (2.0 * math.pi / 987.0)
    rows = np.stack([radius * np.cos(azimuth), radius * np.sin(azimuth), height, np.ones(M)], axis=1)
    share = -(-M // shards)
    padded = -(-share // GROUP) * GROUP
    table = np.zeros((shards, padded, LANES), np.float32)
    for shard in range(shards):
        part = rows[shard * share : (shard + 1) * share]
        table[shard, : part.shape[0], :4] = part
    return table.reshape(shards, padded // GROUP, GROUP, LANES)


def dot(a, b, contract_a, contract_b, precision=None):
    return lax.dot_general(
        a, b, (((contract_a,), (contract_b,)), ((), ())), preferred_element_type=F32, precision=precision
    )


def split2(value):
    high = value.astype(BF16)
    return high, (value - high.astype(F32)).astype(BF16)


def split3(value):
    high = value.astype(BF16).astype(F32)
    rest = value - high
    middle = rest.astype(BF16).astype(F32)
    return high, middle, rest - middle


def sincos(angle):
    turns = jnp.floor(angle * (2.0 / math.pi) + 0.5)
    rest = angle - turns * 1.5703125
    rest = rest - turns * 4.837512969970703125e-4
    rest = rest - turns * 7.54978995489188216e-8
    square = rest * rest
    sine = rest + rest * square * (
        -1.6666654611e-1 + square * (8.3321608736e-3 - square * 1.9515295891e-4)
    )
    cosine = 1.0 - 0.5 * square + square * square * (
        4.166664568298827e-2 + square * (-1.388731625493765e-3 + square * 2.443315711809948e-5)
    )
    quadrant = turns.astype(jnp.int32)
    odd = (quadrant & 1) == 1
    first = jnp.where(odd, sine, cosine)
    second = jnp.where(odd, cosine, sine)
    first = jnp.where(((quadrant + 1) & 2) == 2, -first, first)
    second = jnp.where((quadrant & 2) == 2, -second, second)
    return first, second


def kernel(
    dims,
    fourth_ref,
    pos_ref,
    vel_ref,
    strength_ref,
    mass_ref,
    solute_ref,
    weight_ref,
    shell_ref,
    table_ref,
    pos_out,
    vel_out,
    states,
    halo_left,
    halo_right,
    speed,
    factor,
    near,
    own,
    points,
    level_sp,
    level_rep,
    kick_out,
    kick_in,
    e_high,
    e_low,
    f_high,
    f_low,
    amp_real,
    amp_imag,
    level,
    gains,
    kick_sum,
    halo_send,
    halo_recv,
    point_send,
    point_recv,
    sp_send,
    sp_recv,
    rep_send,
    rep_recv,
    kick_send,
    kick_recv,
):
    count, replicas, blocks, slots, coarse, fine, groups = dims
    rim = blocks // 2
    me = lax.axis_index("sp")
    rep = lax.axis_index("rep")
    q_step = 3.0 / (coarse * fine)
    all_slots = count * slots
    e_half = coarse * GROUP
    f_half = fine * GROUP

    def sp_peer(distance):
        return (rep, lax.rem(me + distance, count))

    def rep_peer(distance):
        return (lax.rem(rep + distance, replicas), me)

    barrier = pltpu.get_barrier_semaphore()
    for distance in range(1, count):
        pl.semaphore_signal(barrier, inc=1, device_id=sp_peer(distance), device_id_type=MESH)
    for distance in range(1, replicas):
        pl.semaphore_signal(barrier, inc=1, device_id=rep_peer(distance), device_id_type=MESH)

    for block in range(blocks):
        span = slice(block * LANES, (block + 1) * LANES)
        strength = strength_ref[:, span]
        states[0, block] = jnp.concatenate(
            [pos_ref[0, :, span], jnp.log(strength), jnp.ones((1, LANES), F32), jnp.zeros((3, LANES), F32)], axis=0
        )
        speed[block] = jnp.concatenate([vel_ref[0, :, span], jnp.zeros((5, LANES), F32)], axis=0)
        coupling = TIME_STEP * PAIR_STRENGTH / math.sqrt(4 * LANES)
        push = jnp.broadcast_to(coupling * strength * mass_ref[:, span], (3, LANES))
        factor[block] = jnp.concatenate([push, jnp.zeros((5, LANES), F32)], axis=0)

    @pl.when(me == 0)
    def _():
        halo_left[...] = jnp.zeros_like(halo_left)

    @pl.when(me == count - 1)
    def _():
        halo_right[...] = jnp.zeros_like(halo_right)

    pl.semaphore_wait(barrier, count - 1 + replicas - 1)

    def halo_copies(step):
        to_right = pltpu.make_async_remote_copy(
            src_ref=states.at[step, pl.ds(blocks - rim, rim)],
            dst_ref=halo_left.at[step],
            send_sem=halo_send.at[step, 0],
            recv_sem=halo_recv.at[step, 0],
            device_id=sp_peer(1),
            device_id_type=MESH,
        )
        to_left = pltpu.make_async_remote_copy(
            src_ref=states.at[step, pl.ds(0, rim)],
            dst_ref=halo_right.at[step],
            send_sem=halo_send.at[step, 1],
            recv_sem=halo_recv.at[step, 1],
            device_id=sp_peer(count - 1),
            device_id_type=MESH,
        )
        return to_right, to_left

    def start_halo(step):
        to_right, to_left = halo_copies(step)
        pl.when(me < count - 1)(to_right.start)
        pl.when(me > 0)(to_left.start)

    def finish_halo(step):
        to_right, to_left = halo_copies(step)
        pl.when(me < count - 1)(to_right.wait_send)
        pl.when(me > 0)(to_left.wait_send)
        pl.when(me > 0)(to_right.wait_recv)
        pl.when(me < count - 1)(to_left.wait_recv)

    def group_copies(source, target, send, recv, outer, peer, size):
        return [
            pltpu.make_async_remote_copy(
                src_ref=source(distance),
                dst_ref=target,
                send_sem=send.at[outer, distance],
                recv_sem=recv.at[outer, distance],
                device_id=peer(distance),
                device_id_type=MESH,
            )
            for distance in range(1, size)
        ]

    def start_all(copies):
        for copy in copies:
            copy.start()

    def wait_all(copies):
        for copy in copies:
            copy.wait()

    row = lax.broadcasted_iota(jnp.int32, (1, 8, LANES), 1)

    def block_features(state):
        radius = HALF_INVERSE * jnp.sum(jnp.where(row < 3, state * state, 0.0), axis=1, keepdims=True)
        return radius, jnp.where(row == 3, state - radius, state)

    def near_features(target, state):
        radius, value = block_features(state)
        high, middle, low = split3(value)
        near[pl.ds(target, state.shape[0])] = jnp.concatenate(
            [high, middle, high, middle, low, high], axis=1
        ).astype(BF16)

    def own_features(index, state):
        radius, value = block_features(state)
        near_side = jnp.where(row < 3, state * (2.0 * HALF_INVERSE), 0.0)
        value = near_side + jnp.where(row == 3, 1.0, 0.0) - jnp.where(row == 4, radius, 0.0)
        high, middle, low = split3(value)
        rows = jnp.concatenate([high, high, middle, middle, high, low], axis=1)
        for k in range(state.shape[0]):
            own[index + k] = rows[k].T.astype(BF16)

    chunk = 4

    def build_own(step):
        @pl.loop(0, blocks // chunk)
        def _(i):
            state = states[step, pl.ds(i * chunk, chunk)]
            near_features(rim + i * chunk, state)
            own_features(i * chunk, state)

    def build_halo(step):
        @pl.loop(0, rim // chunk)
        def _(i):
            near_features(i * chunk, halo_left[step, pl.ds(i * chunk, chunk)])
            near_features(rim + blocks + i * chunk, halo_right[step, pl.ds(i * chunk, chunk)])

    def pair_step(step):
        def one(block):
            sides = [near[block], near[block + rim], near[block + 2 * rim], near[fourth_ref[step, block]]]
            features = jnp.concatenate(sides, axis=1)
            weight = jnp.exp(dot(own[block], features, 1, 0)).astype(BF16)
            sums = dot(features[:16], weight, 1, 1)
            sums = sums[:8] + sums[8:]
            state = states[step, block]
            velocity = speed[block] + factor[block] * (state * sums[4:5] - sums)
            speed[block] = velocity
            states[step + 1, block] = state + TIME_STEP * velocity

        unroll = 4

        @pl.loop(0, blocks // unroll)
        def _(i):
            for k in range(unroll):
                one(i * unroll + k)

    slot_index = solute_ref[...]
    pick_block = (lax.broadcasted_iota(jnp.int32, (blocks, slots), 0) == slot_index // LANES)
    pick_lane = (lax.broadcasted_iota(jnp.int32, (LANES, slots), 0) == slot_index % LANES)
    block_hot = pick_block.astype(F32)
    lane_hot = pick_lane.astype(F32)

    def gather_points(step, outer):
        found = []
        for axis in range(3):
            plane = states[step, :, axis, :].T
            parts = split3(plane)
            spread = sum(dot(part.astype(BF16), block_hot.astype(BF16), 1, 0) for part in parts)
            found.append(jnp.sum(spread * lane_hot, axis=0, keepdims=True))
        points[outer, me] = jnp.concatenate(
            found + [weight_ref[...], jnp.zeros((4, slots), F32)], axis=0
        )

    def amplitudes(outer):
        level[...] = jnp.zeros_like(level)
        width = slots

        @pl.loop(0, groups)
        def _(g):
            directions = table_ref[me, g]
            for part in range(count):
                span = slice(part * width, (part + 1) * width)
                spot = points[outer, part]
                project = (
                    directions[:, 0:1] * spot[0:1] + directions[:, 1:2] * spot[1:2] + directions[:, 2:3] * spot[2:3]
                )

                def put(high_ref, low_ref, at, value):
                    high, low = split2(value)
                    high_ref[g, at : at + GROUP, span] = high
                    low_ref[g, at : at + GROUP, span] = low

                step_cos, step_sin = sincos(q_step * project)
                twice = 2.0 * step_cos
                old = (jnp.ones_like(project), jnp.zeros_like(project))
                new = (step_cos, step_sin)
                for b in range(fine):
                    put(f_high, f_low, b * GROUP, old[0])
                    put(f_high, f_low, f_half + b * GROUP, old[1])
                    old, new = new, (twice * new[0] - old[0], twice * new[1] - old[1])
                jump_cos, jump_sin = old
                real, imag = sincos(project)
                scale = spot[3:4] * directions[:, 3:4]
                real, imag = real * scale, imag * scale
                for a in range(coarse):
                    put(e_high, e_low, a * GROUP, real)
                    put(e_high, e_low, e_half + a * GROUP, imag)
                    real, imag = real * jump_cos - imag * jump_sin, real * jump_sin + imag * jump_cos
            total = (
                dot(e_high[g], f_high[g], 1, 1) + dot(e_high[g], f_low[g], 1, 1) + dot(e_low[g], f_high[g], 1, 1)
            )
            real = total[:e_half, :f_half] - total[e_half:, f_half:]
            imag = total[e_half:, :f_half] + total[:e_half, f_half:]
            amp_real[g] = real
            amp_imag[g] = imag
            level[...] += real * real + imag * imag

        diagonal = diagonal_mask()
        kept = jnp.where(diagonal, level[...], 0.0)
        sums = [jnp.sum(kept[a * GROUP : (a + 1) * GROUP], axis=0, keepdims=True) for a in range(coarse)]
        level_sp[outer, me] = jnp.concatenate(sums + [jnp.zeros((8 - coarse, f_half), F32)], axis=0)

    def diagonal_mask():
        rows = lax.broadcasted_iota(jnp.int32, (e_half, f_half), 0)
        columns = lax.broadcasted_iota(jnp.int32, (e_half, f_half), 1)
        return rows % GROUP == columns % GROUP

    def shell_gains(outer):
        total = level_rep[outer, 0]
        for k in range(1, replicas):
            total = total + level_rep[outer, k]
        rows = lax.broadcasted_iota(jnp.int32, (f_half, f_half), 0)
        columns = lax.broadcasted_iota(jnp.int32, (f_half, f_half), 1)
        same = (rows // GROUP == columns // GROUP).astype(F32)
        shells = dot(total, same, 1, 0, lax.Precision.HIGHEST) / (all_slots * M * replicas)
        coefficient = shell_ref[2] * shell_ref[1] * (shells - shell_ref[0])
        wide = jnp.concatenate(
            [jnp.broadcast_to(coefficient[a : a + 1], (GROUP, f_half)) for a in range(coarse)], axis=0
        )
        gains[...] = jnp.where(diagonal_mask(), wide, 0.0)

    def kicks(outer):
        kick_sum[...] = jnp.zeros_like(kick_sum)

        @pl.loop(0, groups)
        def _(g):
            real = gains[...] * amp_real[g]
            imag = gains[...] * amp_imag[g]
            mixed = jnp.concatenate(
                [jnp.concatenate([real, imag], axis=1), jnp.concatenate([imag, -real], axis=1)], axis=0
            )
            high, low = split2(mixed)
            directions = table_ref[me, g]
            for part in range(count):
                span = slice(part * slots, (part + 1) * slots)
                shells_high = f_high[g, :, span]
                turned = (
                    dot(high, shells_high, 1, 0) + dot(low, shells_high, 1, 0) + dot(high, f_low[g, :, span], 1, 0)
                )
                waves = e_high[g, :, span].astype(F32) + e_low[g, :, span].astype(F32)
                force = jnp.zeros((GROUP, slots), F32)
                for a in range(coarse):
                    here = slice(a * GROUP, (a + 1) * GROUP)
                    there = slice(e_half + a * GROUP, e_half + (a + 1) * GROUP)
                    force = force + waves[here] * turned[there] - waves[there] * turned[here]
                for axis in range(3):
                    kick_sum[axis, :, span] += directions[:, axis : axis + 1] * force

        for part in range(count):
            span = slice(part * slots, (part + 1) * slots)
            sums = [-jnp.sum(kick_sum[axis, :, span], axis=0, keepdims=True) for axis in range(3)]
            kick_out[outer, part] = jnp.concatenate(sums + [jnp.zeros((5, slots), F32)], axis=0)

    def apply_kicks(outer):
        total = kick_in[outer, 0]
        for k in range(1, count):
            total = total + kick_in[outer, k]
        lanes = lane_hot.astype(BF16)
        for axis in range(3):
            parts = split3(total[axis : axis + 1] * block_hot)
            spread = sum(dot(part.astype(BF16), lanes, 1, 1) for part in parts)
            for block in range(blocks):
                mass = mass_ref[:, block * LANES : (block + 1) * LANES]
                speed[block, axis : axis + 1] += (INNER * TIME_STEP) * mass * spread[block : block + 1]

    start_halo(0)
    for outer in range(OUTER):
        first = outer * INNER
        gather_points(first, outer)
        point_copies = group_copies(
            lambda d: points.at[outer, me], points.at[outer, me], point_send, point_recv, outer, sp_peer, count
        )
        start_all(point_copies)
        build_own(first)
        wait_all(point_copies)
        amplitudes(outer)
        sp_copies = group_copies(
            lambda d: level_sp.at[outer, me], level_sp.at[outer, me], sp_send, sp_recv, outer, sp_peer, count
        )
        start_all(sp_copies)
        finish_halo(first)
        build_halo(first)
        wait_all(sp_copies)
        total = level_sp[outer, 0]
        for k in range(1, count):
            total = total + level_sp[outer, k]
        level_rep[outer, rep] = total
        rep_copies = group_copies(
            lambda d: level_rep.at[outer, rep], level_rep.at[outer, rep], rep_send, rep_recv, outer, rep_peer, replicas
        )
        start_all(rep_copies)
        pair_step(first)
        for inner in range(1, INNER):
            step = first + inner
            start_halo(step)
            build_own(step)
            if inner == 1:
                wait_all(rep_copies)
                shell_gains(outer)
                kicks(outer)
                kick_in[outer, me] = kick_out[outer, me]
                kick_copies = group_copies(
                    lambda d: kick_out.at[outer, lax.rem(me + d, count)],
                    kick_in.at[outer, me],
                    kick_send,
                    kick_recv,
                    outer,
                    sp_peer,
                    count,
                )
                start_all(kick_copies)
            finish_halo(step)
            build_halo(step)
            pair_step(step)
        if outer + 1 < OUTER:
            start_halo(first + INNER)
        wait_all(kick_copies)
        apply_kicks(outer)

    for block in range(blocks):
        span = slice(block * LANES, (block + 1) * LANES)
        pos_out[0, :, span] = states[OUTER * INNER, block, 0:3]
        vel_out[0, :, span] = speed[block, 0:3]


def solution(mesh):
    count, replicas = mesh.shape["sp"], mesh.shape["rep"]
    table = direction_table(count)
    groups = table.shape[1]
    steps = OUTER * INNER

    def shards(
        positions, velocities, strength, inv_mass, tile_lists, solute_index, scatter_weight, intensity_exp, precision
    ):
        atoms = positions.shape[2]
        blocks = atoms // LANES
        rim = blocks // 2
        slots = solute_index.shape[1]
        shells = intensity_exp.shape[0]
        fine = LANES // GROUP
        coarse = shells // fine
        order = jnp.arange(blocks, dtype=jnp.int32)
        fourth = jnp.sum(tile_lists[0], axis=-1) - 3 * (order + rim)[None, :]
        q = 1.0 + 3.0 * jnp.arange(shells, dtype=F32) / shells
        gain = 2.0 * precision * q / (M * math.sqrt(count * slots))
        rows = jnp.stack([intensity_exp, gain, jnp.ones_like(q)]).reshape(3, coarse, fine)
        rows = jnp.pad(jnp.repeat(rows, GROUP, axis=2), ((0, 0), (0, 8 - coarse), (0, 0)))
        e_rows, f_rows, wide = 2 * coarse * GROUP, 2 * fine * GROUP, count * slots
        vmem = pl.BlockSpec(memory_space=pltpu.VMEM)
        dma = pltpu.SemaphoreType.DMA
        return pl.pallas_call(
            functools.partial(kernel, (count, replicas, blocks, slots, coarse, fine, groups)),
            out_shape=(
                jax.ShapeDtypeStruct(positions.shape, F32),
                jax.ShapeDtypeStruct(velocities.shape, F32),
            ),
            in_specs=[pl.BlockSpec(memory_space=pltpu.SMEM)] + [vmem] * 8,
            out_specs=(vmem, vmem),
            scratch_shapes=[
                pltpu.VMEM((steps + 1, blocks, 8, LANES), F32),
                pltpu.VMEM((steps, rim, 8, LANES), F32),
                pltpu.VMEM((steps, rim, 8, LANES), F32),
                pltpu.VMEM((blocks, 8, LANES), F32),
                pltpu.VMEM((blocks, 8, LANES), F32),
                pltpu.VMEM((2 * blocks, ROWS, LANES), BF16),
                pltpu.VMEM((blocks, LANES, ROWS), BF16),
                pltpu.VMEM((OUTER, count, 8, slots), F32),
                pltpu.VMEM((OUTER, count, 8, LANES), F32),
                pltpu.VMEM((OUTER, replicas, 8, LANES), F32),
                pltpu.VMEM((OUTER, count, 8, slots), F32),
                pltpu.VMEM((OUTER, count, 8, slots), F32),
                pltpu.VMEM((groups, e_rows, wide), BF16),
                pltpu.VMEM((groups, e_rows, wide), BF16),
                pltpu.VMEM((groups, f_rows, wide), BF16),
                pltpu.VMEM((groups, f_rows, wide), BF16),
                pltpu.VMEM((groups, e_rows // 2, f_rows // 2), F32),
                pltpu.VMEM((groups, e_rows // 2, f_rows // 2), F32),
                pltpu.VMEM((e_rows // 2, f_rows // 2), F32),
                pltpu.VMEM((e_rows // 2, f_rows // 2), F32),
                pltpu.VMEM((3, GROUP, wide), F32),
                dma((steps, 2)),
                dma((steps, 2)),
                dma((OUTER, count)),
                dma((OUTER, count)),
                dma((OUTER, count)),
                dma((OUTER, count)),
                dma((OUTER, replicas)),
                dma((OUTER, replicas)),
                dma((OUTER, count)),
                dma((OUTER, count)),
            ],
            compiler_params=pltpu.CompilerParams(
                collective_id=0, has_side_effects=True, vmem_limit_bytes=58 * 1024 * 1024
            ),
            cost_estimate=pl.CostEstimate(flops=40_000_000_000, bytes_accessed=4_000_000, transcendentals=20_000_000),
        )(fourth, positions, velocities, strength, inv_mass, solute_index, scatter_weight, rows, jnp.asarray(table))

    in_specs = (
        P("rep", None, "sp"),
        P("rep", None, "sp"),
        P("rep", "sp"),
        P("rep", "sp"),
        P("rep", None, "sp", None),
        P("rep", "sp"),
        P("rep", "sp"),
        P(),
        P(),
    )
    out_specs = (P("rep", None, "sp"), P("rep", None, "sp"))
    return jax.shard_map(shards, mesh=mesh, in_specs=in_specs, out_specs=out_specs, check_vma=False)
```

```python
import functools
import math

import jax
import jax.numpy as jnp
import numpy as np
from jax import lax
from jax.experimental import pallas as pl
from jax.experimental.pallas import tpu as pltpu
from jax.sharding import PartitionSpec as P

M = 784
OUTER = 2
INNER = 2
TIME_STEP = 0.05
PAIR_STRENGTH = 0.2
HALF_INVERSE = 0.03125
LANES = 128
GROUP = 16
ROWS = 48
F32 = jnp.float32
BF16 = jnp.bfloat16
MESH = pl.DeviceIdType.MESH


def direction_table(shards):
    order = np.arange(M)
    height = 1.0 - (2.0 * order + 1.0) / M
    radius = np.sqrt(1.0 - height * height)
    azimuth = (order * 610 % 987) * (2.0 * math.pi / 987.0)
    rows = np.stack([radius * np.cos(azimuth), radius * np.sin(azimuth), height, np.ones(M)], axis=1)
    share = -(-M // shards)
    padded = -(-share // GROUP) * GROUP
    table = np.zeros((shards, padded, LANES), np.float32)
    for shard in range(shards):
        part = rows[shard * share : (shard + 1) * share]
        table[shard, : part.shape[0], :4] = part
    return table.reshape(shards, padded // GROUP, GROUP, LANES)


def dot(a, b, contract_a, contract_b, precision=None):
    return lax.dot_general(
        a, b, (((contract_a,), (contract_b,)), ((), ())), preferred_element_type=F32, precision=precision
    )


def split2(value):
    high = value.astype(BF16)
    return high, (value - high.astype(F32)).astype(BF16)


def split3(value):
    high = value.astype(BF16).astype(F32)
    rest = value - high
    middle = rest.astype(BF16).astype(F32)
    return high, middle, rest - middle


def sincos(angle):
    turns = jnp.floor(angle * (2.0 / math.pi) + 0.5)
    rest = angle - turns * 1.5703125
    rest = rest - turns * 4.837512969970703125e-4
    rest = rest - turns * 7.54978995489188216e-8
    square = rest * rest
    sine = rest + rest * square * (
        -1.6666654611e-1 + square * (8.3321608736e-3 - square * 1.9515295891e-4)
    )
    cosine = 1.0 - 0.5 * square + square * square * (
        4.166664568298827e-2 + square * (-1.388731625493765e-3 + square * 2.443315711809948e-5)
    )
    quadrant = turns.astype(jnp.int32)
    odd = (quadrant & 1) == 1
    first = jnp.where(odd, sine, cosine)
    second = jnp.where(odd, cosine, sine)
    first = jnp.where(((quadrant + 1) & 2) == 2, -first, first)
    second = jnp.where((quadrant & 2) == 2, -second, second)
    return first, second


def kernel(
    dims,
    tile_ref,
    pos_ref,
    vel_ref,
    strength_ref,
    mass_ref,
    solute_ref,
    weight_ref,
    target_ref,
    precision_ref,
    table_ref,
    pos_out,
    vel_out,
    states,
    halo_left,
    halo_right,
    speed,
    factor,
    near_even,
    near_odd,
    own_even,
    own_odd,
    points,
    level_sp,
    level_rep,
    kick_out,
    kick_in,
    e_high,
    e_low,
    f_high,
    f_low,
    amp_real,
    amp_imag,
    level,
    gains,
    kick_sum,
    halo_send,
    halo_recv,
    point_send,
    point_recv,
    sp_send,
    sp_recv,
    rep_send,
    rep_recv,
    kick_send,
    kick_recv,
):
    count, replicas, blocks, slots, coarse, fine, groups = dims
    rim = blocks // 2
    me = lax.axis_index("sp")
    rep = lax.axis_index("rep")
    q_step = 3.0 / (coarse * fine)
    all_slots = count * slots
    e_half = coarse * GROUP
    f_half = fine * GROUP

    def sp_peer(distance):
        return (rep, lax.rem(me + distance, count))

    def rep_peer(distance):
        return (lax.rem(rep + distance, replicas), me)

    barrier = pltpu.get_barrier_semaphore()
    for distance in range(1, count):
        pl.semaphore_signal(barrier, inc=1, device_id=sp_peer(distance), device_id_type=MESH)
    for distance in range(1, replicas):
        pl.semaphore_signal(barrier, inc=1, device_id=rep_peer(distance), device_id_type=MESH)

    row = lax.broadcasted_iota(jnp.int32, (1, 8, LANES), 1)
    strength = strength_ref[...]
    push = (TIME_STEP * PAIR_STRENGTH / math.sqrt(4 * LANES)) * strength * mass_ref[...]
    states[0] = jnp.broadcast_to(jnp.where(row == 4, 1.0, 0.0), (blocks, 8, LANES))
    speed[...] = jnp.zeros_like(speed)
    factor[...] = jnp.zeros_like(factor)
    states[0, :, 3, :] = jnp.log(strength)
    for axis in range(3):
        states[0, :, axis, :] = pos_ref[axis]
        speed[:, axis, :] = vel_ref[axis]
        factor[:, axis, :] = push

    @pl.when(me == 0)
    def _():
        halo_left[...] = jnp.zeros_like(halo_left)

    @pl.when(me == count - 1)
    def _():
        halo_right[...] = jnp.zeros_like(halo_right)

    pl.semaphore_wait(barrier, count - 1 + replicas - 1)

    def halo_copies(step):
        to_right = pltpu.make_async_remote_copy(
            src_ref=states.at[step, pl.ds(blocks - rim, rim)],
            dst_ref=halo_left.at[step],
            send_sem=halo_send.at[step, 0],
            recv_sem=halo_recv.at[step, 0],
            device_id=sp_peer(1),
            device_id_type=MESH,
        )
        to_left = pltpu.make_async_remote_copy(
            src_ref=states.at[step, pl.ds(0, rim)],
            dst_ref=halo_right.at[step],
            send_sem=halo_send.at[step, 1],
            recv_sem=halo_recv.at[step, 1],
            device_id=sp_peer(count - 1),
            device_id_type=MESH,
        )
        return to_right, to_left

    def start_halo(step):
        to_right, to_left = halo_copies(step)
        pl.when(me < count - 1)(to_right.start)
        pl.when(me > 0)(to_left.start)

    def finish_halo(step):
        to_right, to_left = halo_copies(step)
        pl.when(me < count - 1)(to_right.wait_send)
        pl.when(me > 0)(to_left.wait_send)
        pl.when(me > 0)(to_right.wait_recv)
        pl.when(me < count - 1)(to_left.wait_recv)

    def group_copies(source, target, send, recv, outer, peer, size):
        return [
            pltpu.make_async_remote_copy(
                src_ref=source(distance),
                dst_ref=target,
                send_sem=send.at[outer, distance],
                recv_sem=recv.at[outer, distance],
                device_id=peer(distance),
                device_id_type=MESH,
            )
            for distance in range(1, size)
        ]

    def start_all(copies):
        for copy in copies:
            copy.start()

    def wait_all(copies):
        for copy in copies:
            copy.wait()

    def block_features(state):
        radius = HALF_INVERSE * jnp.sum(jnp.where(row < 3, state * state, 0.0), axis=1, keepdims=True)
        return radius, jnp.where(row == 3, state - radius, state)

    def near_features(near, target, state):
        radius, value = block_features(state)
        high, middle, low = split3(value)
        near[pl.ds(target, state.shape[0])] = jnp.concatenate(
            [high, middle, high, middle, low, high], axis=1
        ).astype(BF16)

    def own_features(own, index, state):
        radius, value = block_features(state)
        near_side = jnp.where(row < 3, state * (2.0 * HALF_INVERSE), 0.0)
        value = near_side + jnp.where(row == 3, 1.0, 0.0) - jnp.where(row == 4, radius, 0.0)
        high, middle, low = split3(value)
        rows = jnp.concatenate([high, high, middle, middle, high, low], axis=1)
        for k in range(state.shape[0]):
            own[index + k] = rows[k].T.astype(BF16)

    chunk = 8
    nears, owns = (near_even, near_odd), (own_even, own_odd)

    def build_own(step):
        @pl.loop(0, blocks // chunk)
        def _(i):
            state = states[step, pl.ds(i * chunk, chunk)]
            near_features(nears[step % 2], rim + i * chunk, state)
            own_features(owns[step % 2], i * chunk, state)

    def build_halo(step):
        @pl.loop(0, rim // chunk)
        def _(i):
            near_features(nears[step % 2], i * chunk, halo_left[step, pl.ds(i * chunk, chunk)])
            near_features(nears[step % 2], rim + blocks + i * chunk, halo_right[step, pl.ds(i * chunk, chunk)])

    def pair_step(step):
        near, own = nears[step % 2], owns[step % 2]
        near_next, own_next = nears[(step + 1) % 2], owns[(step + 1) % 2]

        def one(block):
            fourth = tile_ref[step, 0, block] + tile_ref[step, 1, block] + tile_ref[step, 2, block]
            fourth = fourth + tile_ref[step, 3, block] - 3 * (block + rim)
            fourth = jnp.clip(fourth, 0, 2 * blocks - 1)
            mine = own[block]
            sums = jnp.zeros((16, LANES), F32)
            for pair in ((block, block + rim), (block + 2 * rim, fourth)):
                features = jnp.concatenate([near[pair[0]], near[pair[1]]], axis=1)
                weight = jnp.exp(dot(mine, features, 1, 0)).astype(BF16)
                sums = sums + dot(features[:16], weight, 1, 1)
            sums = sums[:8] + sums[8:]
            state = states[step, block]
            velocity = speed[block] + factor[block] * (state * sums[4:5] - sums)
            speed[block] = velocity
            state = state + TIME_STEP * velocity
            states[step + 1, block] = state
            if step + 1 < OUTER * INNER:
                near_features(near_next, rim + block, state[None])
                own_features(own_next, block, state[None])

        unroll = 8 if blocks % 8 == 0 else 1

        @pl.loop(0, blocks // unroll)
        def _(i):
            for k in range(unroll):
                one(i * unroll + k)

    slot_index = solute_ref[...]
    pick_block = (lax.broadcasted_iota(jnp.int32, (blocks, slots), 0) == slot_index // LANES)
    pick_lane = (lax.broadcasted_iota(jnp.int32, (LANES, slots), 0) == slot_index % LANES)
    block_hot = pick_block.astype(F32)
    lane_hot = pick_lane.astype(F32)

    def gather_points(step, outer):
        found = []
        for axis in range(3):
            plane = states[step, :, axis, :].T
            parts = split3(plane)
            spread = sum(dot(part.astype(BF16), block_hot.astype(BF16), 1, 0) for part in parts)
            found.append(jnp.sum(spread * lane_hot, axis=0, keepdims=True))
        points[outer, me] = jnp.concatenate(
            found + [weight_ref[...], jnp.zeros((4, slots), F32)], axis=0
        )

    def amplitudes(outer):
        level[...] = jnp.zeros_like(level)
        width = slots

        @pl.loop(0, groups)
        def _(g):
            directions = table_ref[me, g]
            total = jnp.zeros((2 * e_half, 2 * f_half), F32)
            for part in range(count):
                span = slice(part * width, (part + 1) * width)
                spot = points[outer, part]
                project = (
                    directions[:, 0:1] * spot[0:1] + directions[:, 1:2] * spot[1:2] + directions[:, 2:3] * spot[2:3]
                )

                def put(high_ref, low_ref, at, value):
                    high, low = split2(value)
                    high_ref[g, at : at + GROUP, span] = high
                    low_ref[g, at : at + GROUP, span] = low

                step_cos, step_sin = sincos(q_step * project)
                twice = 2.0 * step_cos
                old = (jnp.ones_like(project), jnp.zeros_like(project))
                new = (step_cos, step_sin)
                for b in range(fine):
                    put(f_high, f_low, b * GROUP, old[0])
                    put(f_high, f_low, f_half + b * GROUP, old[1])
                    old, new = new, (twice * new[0] - old[0], twice * new[1] - old[1])
                jump_cos, jump_sin = old
                if 3 * 2 * fine == coarse * fine:
                    real, imag = jump_cos * jump_cos - jump_sin * jump_sin, 2.0 * jump_cos * jump_sin
                else:
                    real, imag = sincos(project)
                scale = spot[3:4] * directions[:, 3:4]
                real, imag = real * scale, imag * scale
                for a in range(coarse):
                    put(e_high, e_low, a * GROUP, real)
                    put(e_high, e_low, e_half + a * GROUP, imag)
                    real, imag = real * jump_cos - imag * jump_sin, real * jump_sin + imag * jump_cos
                waves, bands = e_high[g, :, span], f_high[g, :, span]
                waves = jnp.concatenate([waves, waves, e_low[g, :, span]], axis=1)
                bands = jnp.concatenate([bands, f_low[g, :, span], bands], axis=1)
                total = total + dot(waves, bands, 1, 1)
            real = total[:e_half, :f_half] - total[e_half:, f_half:]
            imag = total[e_half:, :f_half] + total[:e_half, f_half:]
            amp_real[g] = real
            amp_imag[g] = imag
            level[...] += real * real + imag * imag

        diagonal = diagonal_mask()
        kept = jnp.where(diagonal, level[...], 0.0)
        sums = [jnp.sum(kept[a * GROUP : (a + 1) * GROUP], axis=0, keepdims=True) for a in range(coarse)]
        level_sp[outer, me] = jnp.concatenate(sums + [jnp.zeros((8 - coarse, f_half), F32)], axis=0)

    def diagonal_mask():
        rows = lax.broadcasted_iota(jnp.int32, (e_half, f_half), 0)
        columns = lax.broadcasted_iota(jnp.int32, (e_half, f_half), 1)
        return rows % GROUP == columns % GROUP

    def shell_gains(outer):
        total = level_rep[outer, 0]
        for k in range(1, replicas):
            total = total + level_rep[outer, k]
        rows = lax.broadcasted_iota(jnp.int32, (f_half, f_half), 0)
        columns = lax.broadcasted_iota(jnp.int32, (f_half, f_half), 1)
        same = (rows // GROUP == columns // GROUP).astype(F32)
        shells = dot(total, same, 1, 0, lax.Precision.HIGHEST) / (all_slots * M * replicas)
        count_shells = coarse * fine
        shell = lax.broadcasted_iota(jnp.int32, (8, count_shells), 1)
        in_row = shell // fine == lax.broadcasted_iota(jnp.int32, (8, count_shells), 0)
        shell = lax.broadcasted_iota(jnp.int32, (count_shells, f_half), 0)
        in_lane = shell % fine == lax.broadcasted_iota(jnp.int32, (count_shells, f_half), 1) // GROUP

        def spread(values):
            rows = jnp.where(in_row, values, 0.0)
            return dot(rows, in_lane.astype(F32), 1, 0, lax.Precision.HIGHEST)

        order = lax.broadcasted_iota(jnp.int32, (1, count_shells), 1).astype(F32)
        gain = precision_ref[...] * (1.0 + q_step * order) * (2.0 / (M * math.sqrt(all_slots)))
        coefficient = spread(gain) * (shells - spread(target_ref[...]))
        wide = jnp.concatenate(
            [jnp.broadcast_to(coefficient[a : a + 1], (GROUP, f_half)) for a in range(coarse)], axis=0
        )
        gains[...] = jnp.where(diagonal_mask(), wide, 0.0)

    def kicks(outer):
        kick_sum[...] = jnp.zeros_like(kick_sum)

        @pl.loop(0, groups)
        def _(g):
            real = gains[...] * amp_real[g]
            imag = gains[...] * amp_imag[g]
            mixed = jnp.concatenate(
                [jnp.concatenate([real, imag], axis=1), jnp.concatenate([imag, -real], axis=1)], axis=0
            )
            high, low = split2(mixed)
            mixed = jnp.concatenate([high, low, high], axis=1)
            directions = table_ref[me, g]
            for part in range(count):
                span = slice(part * slots, (part + 1) * slots)
                bands = f_high[g, :, span]
                turned = dot(mixed, jnp.concatenate([bands, bands, f_low[g, :, span]], axis=0), 1, 0)
                waves = e_high[g, :, span].astype(F32) + e_low[g, :, span].astype(F32)
                force = jnp.zeros((GROUP, slots), F32)
                for a in range(coarse):
                    here = slice(a * GROUP, (a + 1) * GROUP)
                    there = slice(e_half + a * GROUP, e_half + (a + 1) * GROUP)
                    force = force + waves[here] * turned[there] - waves[there] * turned[here]
                for axis in range(3):
                    kick_sum[axis, :, span] += directions[:, axis : axis + 1] * force

        for part in range(count):
            span = slice(part * slots, (part + 1) * slots)
            sums = [-jnp.sum(kick_sum[axis, :, span], axis=0, keepdims=True) for axis in range(3)]
            kick_out[outer, part] = jnp.concatenate(sums + [jnp.zeros((5, slots), F32)], axis=0)

    def apply_kicks(outer):
        total = kick_in[outer, 0]
        for k in range(1, count):
            total = total + kick_in[outer, k]
        lanes = lane_hot.astype(BF16)
        for axis in range(3):
            parts = split3(total[axis : axis + 1] * block_hot)
            spread = sum(dot(part.astype(BF16), lanes, 1, 1) for part in parts)
            speed[:, axis, :] = speed[:, axis, :] + (INNER * TIME_STEP) * mass_ref[...] * spread

    start_halo(0)
    kick_copies = []
    for outer in range(OUTER):
        first = outer * INNER
        gather_points(first, outer)
        point_copies = group_copies(
            lambda d: points.at[outer, me], points.at[outer, me], point_send, point_recv, outer, sp_peer, count
        )
        start_all(point_copies)
        if outer == 0:
            build_own(first)
        else:
            wait_all(kick_copies)
            apply_kicks(outer - 1)
            finish_halo(first)
            build_halo(first)
        wait_all(point_copies)
        amplitudes(outer)
        sp_copies = group_copies(
            lambda d: level_sp.at[outer, me], level_sp.at[outer, me], sp_send, sp_recv, outer, sp_peer, count
        )
        start_all(sp_copies)
        if outer == 0:
            finish_halo(first)
            build_halo(first)
        wait_all(sp_copies)
        total = level_sp[outer, 0]
        for k in range(1, count):
            total = total + level_sp[outer, k]
        level_rep[outer, rep] = total
        rep_copies = group_copies(
            lambda d: level_rep.at[outer, rep], level_rep.at[outer, rep], rep_send, rep_recv, outer, rep_peer, replicas
        )
        start_all(rep_copies)
        pair_step(first)
        for inner in range(1, INNER):
            step = first + inner
            start_halo(step)
            if inner == 1:
                wait_all(rep_copies)
                shell_gains(outer)
                kicks(outer)
                kick_in[outer, me] = kick_out[outer, me]
                kick_copies = group_copies(
                    lambda d: kick_out.at[outer, lax.rem(me + d, count)],
                    kick_in.at[outer, me],
                    kick_send,
                    kick_recv,
                    outer,
                    sp_peer,
                    count,
                )
                start_all(kick_copies)
            finish_halo(step)
            build_halo(step)
            pair_step(step)
        if outer + 1 < OUTER:
            start_halo(first + INNER)
    wait_all(kick_copies)
    apply_kicks(OUTER - 1)
    for axis in range(3):
        pos_out[axis] = states[OUTER * INNER, :, axis, :]
        vel_out[axis] = speed[:, axis, :]


def solution(mesh):
    count, replicas = mesh.shape["sp"], mesh.shape["rep"]
    table = direction_table(count)
    groups = table.shape[1]
    steps = OUTER * INNER

    def shards(
        positions, velocities, strength, inv_mass, tile_lists, solute_index, scatter_weight, intensity_exp, precision
    ):
        atoms = positions.shape[2]
        blocks = atoms // LANES
        rim = blocks // 2
        slots = solute_index.shape[1]
        shells = intensity_exp.shape[0]
        fine = LANES // GROUP
        coarse = shells // fine
        planes = (3, blocks, LANES)
        e_rows, f_rows, wide = 2 * coarse * GROUP, 2 * fine * GROUP, count * slots
        vmem = pl.BlockSpec(memory_space=pltpu.VMEM)
        dma = pltpu.SemaphoreType.DMA
        coords, speeds = pl.pallas_call(
            functools.partial(kernel, (count, replicas, blocks, slots, coarse, fine, groups)),
            out_shape=(
                jax.ShapeDtypeStruct(planes, F32),
                jax.ShapeDtypeStruct(planes, F32),
            ),
            in_specs=[pl.BlockSpec(memory_space=pltpu.SMEM)] + [vmem] * 9,
            out_specs=(vmem, vmem),
            scratch_shapes=[
                pltpu.VMEM((steps + 1, blocks, 8, LANES), F32),
                pltpu.VMEM((steps, rim, 8, LANES), F32),
                pltpu.VMEM((steps, rim, 8, LANES), F32),
                pltpu.VMEM((blocks, 8, LANES), F32),
                pltpu.VMEM((blocks, 8, LANES), F32),
                pltpu.VMEM((2 * blocks, ROWS, LANES), BF16),
                pltpu.VMEM((2 * blocks, ROWS, LANES), BF16),
                pltpu.VMEM((blocks, LANES, ROWS), BF16),
                pltpu.VMEM((blocks, LANES, ROWS), BF16),
                pltpu.VMEM((OUTER, count, 8, slots), F32),
                pltpu.VMEM((OUTER, count, 8, LANES), F32),
                pltpu.VMEM((OUTER, replicas, 8, LANES), F32),
                pltpu.VMEM((OUTER, count, 8, slots), F32),
                pltpu.VMEM((OUTER, count, 8, slots), F32),
                pltpu.VMEM((groups, e_rows, wide), BF16),
                pltpu.VMEM((groups, e_rows, wide), BF16),
                pltpu.VMEM((groups, f_rows, wide), BF16),
                pltpu.VMEM((groups, f_rows, wide), BF16),
                pltpu.VMEM((groups, e_rows // 2, f_rows // 2), F32),
                pltpu.VMEM((groups, e_rows // 2, f_rows // 2), F32),
                pltpu.VMEM((e_rows // 2, f_rows // 2), F32),
                pltpu.VMEM((e_rows // 2, f_rows // 2), F32),
                pltpu.VMEM((3, GROUP, wide), F32),
                dma((steps, 2)),
                dma((steps, 2)),
                dma((OUTER, count)),
                dma((OUTER, count)),
                dma((OUTER, count)),
                dma((OUTER, count)),
                dma((OUTER, replicas)),
                dma((OUTER, replicas)),
                dma((OUTER, count)),
                dma((OUTER, count)),
            ],
            compiler_params=pltpu.CompilerParams(
                collective_id=0, has_side_effects=True, vmem_limit_bytes=58 * 1024 * 1024
            ),
            cost_estimate=pl.CostEstimate(flops=40_000_000_000, bytes_accessed=4_000_000, transcendentals=20_000_000),
        )(
            jnp.transpose(tile_lists[0], (0, 2, 1)),
            positions.reshape(planes),
            velocities.reshape(planes),
            strength.reshape(blocks, LANES),
            inv_mass.reshape(blocks, LANES),
            solute_index,
            scatter_weight,
            intensity_exp.reshape(1, shells),
            precision.reshape(1, shells),
            jnp.asarray(table),
        )
        return coords.reshape(positions.shape), speeds.reshape(velocities.shape)

    in_specs = (
        P("rep", None, "sp"),
        P("rep", None, "sp"),
        P("rep", "sp"),
        P("rep", "sp"),
        P("rep", None, "sp", None),
        P("rep", "sp"),
        P("rep", "sp"),
        P(),
        P(),
    )
    out_specs = (P("rep", None, "sp"), P("rep", None, "sp"))
    return jax.shard_map(shards, mesh=mesh, in_specs=in_specs, out_specs=out_specs, check_vma=False)
```

```python
import functools
import math

import jax
import jax.numpy as jnp
import numpy as np
from jax import lax
from jax.experimental import pallas as pl
from jax.experimental.pallas import tpu as pltpu
from jax.sharding import PartitionSpec as P

M = 784
OUTER = 2
INNER = 2
TIME_STEP = 0.05
PAIR_STRENGTH = 0.2
HALF_INVERSE = 0.03125
LANES = 128
GROUP = 16
ROWS = 48
F32 = jnp.float32
BF16 = jnp.bfloat16
MESH = pl.DeviceIdType.MESH


def direction_table(shards):
    order = np.arange(M)
    height = 1.0 - (2.0 * order + 1.0) / M
    radius = np.sqrt(1.0 - height * height)
    azimuth = (order * 610 % 987) * (2.0 * math.pi / 987.0)
    rows = np.stack([radius * np.cos(azimuth), radius * np.sin(azimuth), height, np.ones(M)], axis=1)
    share = -(-M // shards)
    padded = -(-share // GROUP) * GROUP
    table = np.zeros((shards, padded, LANES), np.float32)
    for shard in range(shards):
        part = rows[shard * share : (shard + 1) * share]
        table[shard, : part.shape[0], :4] = part
    return table.reshape(shards, padded // GROUP, GROUP, LANES)


def dot(a, b, contract_a, contract_b, precision=None):
    return lax.dot_general(
        a, b, (((contract_a,), (contract_b,)), ((), ())), preferred_element_type=F32, precision=precision
    )


def split2(value):
    high = value.astype(BF16)
    return high, (value - high.astype(F32)).astype(BF16)


def split3(value):
    high = value.astype(BF16).astype(F32)
    rest = value - high
    middle = rest.astype(BF16).astype(F32)
    return high, middle, rest - middle


def sincos(angle):
    turns = jnp.floor(angle * (2.0 / math.pi) + 0.5)
    rest = angle - turns * 1.5703125
    rest = rest - turns * 4.837512969970703125e-4
    rest = rest - turns * 7.54978995489188216e-8
    square = rest * rest
    sine = rest + rest * square * (
        -1.6666654611e-1 + square * (8.3321608736e-3 - square * 1.9515295891e-4)
    )
    cosine = 1.0 - 0.5 * square + square * square * (
        4.166664568298827e-2 + square * (-1.388731625493765e-3 + square * 2.443315711809948e-5)
    )
    quadrant = turns.astype(jnp.int32)
    odd = (quadrant & 1) == 1
    first = jnp.where(odd, sine, cosine)
    second = jnp.where(odd, cosine, sine)
    first = jnp.where(((quadrant + 1) & 2) == 2, -first, first)
    second = jnp.where((quadrant & 2) == 2, -second, second)
    return first, second


def kernel(
    dims,
    tile_ref,
    pos_ref,
    vel_ref,
    strength_ref,
    mass_ref,
    solute_ref,
    weight_ref,
    target_ref,
    precision_ref,
    table_ref,
    pos_out,
    vel_out,
    states,
    halo_left,
    halo_right,
    speed,
    factor,
    near_even,
    near_odd,
    own_even,
    own_odd,
    points,
    level_sp,
    level_rep,
    kick_out,
    kick_in,
    e_high,
    e_low,
    f_high,
    f_low,
    amp_real,
    amp_imag,
    level,
    gains,
    kick_sum,
    halo_send,
    halo_recv,
    point_send,
    point_recv,
    sp_send,
    sp_recv,
    rep_send,
    rep_recv,
    kick_send,
    kick_recv,
):
    count, replicas, blocks, slots, coarse, fine, groups = dims
    rim = blocks // 2
    me = lax.axis_index("sp")
    rep = lax.axis_index("rep")
    q_step = 3.0 / (coarse * fine)
    all_slots = count * slots
    e_half = coarse * GROUP
    f_half = fine * GROUP

    def sp_peer(distance):
        return (rep, lax.rem(me + distance, count))

    def rep_peer(distance):
        return (lax.rem(rep + distance, replicas), me)

    barrier = pltpu.get_barrier_semaphore()
    for distance in range(1, count):
        pl.semaphore_signal(barrier, inc=1, device_id=sp_peer(distance), device_id_type=MESH)
    for distance in range(1, replicas):
        pl.semaphore_signal(barrier, inc=1, device_id=rep_peer(distance), device_id_type=MESH)

    row = lax.broadcasted_iota(jnp.int32, (1, 8, LANES), 1)
    strength = strength_ref[...]
    push = (TIME_STEP * PAIR_STRENGTH / math.sqrt(4 * LANES)) * strength * mass_ref[...]
    states[0] = jnp.broadcast_to(jnp.where(row == 4, 1.0, 0.0), (blocks, 8, LANES))
    speed[0] = jnp.zeros_like(speed[0])
    factor[...] = jnp.zeros_like(factor)
    states[0, :, 3, :] = jnp.log(strength)
    for axis in range(3):
        states[0, :, axis, :] = pos_ref[axis]
        speed[0, :, axis, :] = vel_ref[axis]
        factor[:, axis, :] = push

    @pl.when(me == 0)
    def _():
        halo_left[...] = jnp.zeros_like(halo_left)

    @pl.when(me == count - 1)
    def _():
        halo_right[...] = jnp.zeros_like(halo_right)

    pl.semaphore_wait(barrier, count - 1 + replicas - 1)

    def halo_copies(step):
        to_right = pltpu.make_async_remote_copy(
            src_ref=states.at[step, pl.ds(blocks - rim, rim)],
            dst_ref=halo_left.at[step],
            send_sem=halo_send.at[step, 0],
            recv_sem=halo_recv.at[step, 0],
            device_id=sp_peer(1),
            device_id_type=MESH,
        )
        to_left = pltpu.make_async_remote_copy(
            src_ref=states.at[step, pl.ds(0, rim)],
            dst_ref=halo_right.at[step],
            send_sem=halo_send.at[step, 1],
            recv_sem=halo_recv.at[step, 1],
            device_id=sp_peer(count - 1),
            device_id_type=MESH,
        )
        return to_right, to_left

    def start_halo(step):
        to_right, to_left = halo_copies(step)
        pl.when(me < count - 1)(to_right.start)
        pl.when(me > 0)(to_left.start)

    def finish_halo(step):
        to_right, to_left = halo_copies(step)
        pl.when(me < count - 1)(to_right.wait_send)
        pl.when(me > 0)(to_left.wait_send)
        pl.when(me > 0)(to_right.wait_recv)
        pl.when(me < count - 1)(to_left.wait_recv)

    def group_copies(source, target, send, recv, outer, peer, size):
        return [
            pltpu.make_async_remote_copy(
                src_ref=source(distance),
                dst_ref=target,
                send_sem=send.at[outer, distance],
                recv_sem=recv.at[outer, distance],
                device_id=peer(distance),
                device_id_type=MESH,
            )
            for distance in range(1, size)
        ]

    def start_all(copies):
        for copy in copies:
            copy.start()

    def wait_all(copies):
        for copy in copies:
            copy.wait()

    def block_features(state):
        radius = HALF_INVERSE * jnp.sum(jnp.where(row < 3, state * state, 0.0), axis=1, keepdims=True)
        return radius, jnp.where(row == 3, state - radius, state)

    def near_features(near, target, state):
        radius, value = block_features(state)
        high, middle, low = split3(value)
        near[pl.ds(target, state.shape[0])] = jnp.concatenate(
            [high, middle, high, middle, low, high], axis=1
        ).astype(BF16)

    def own_features(own, index, state):
        radius, value = block_features(state)
        near_side = jnp.where(row < 3, state * (2.0 * HALF_INVERSE), 0.0)
        value = near_side + jnp.where(row == 3, 1.0, 0.0) - jnp.where(row == 4, radius, 0.0)
        high, middle, low = split3(value)
        rows = jnp.concatenate([high, high, middle, middle, high, low], axis=1)
        for k in range(state.shape[0]):
            own[index + k] = rows[k].T.astype(BF16)

    chunk = 8
    nears, owns = (near_even, near_odd), (own_even, own_odd)

    def build_own(step):
        @pl.loop(0, blocks // chunk)
        def _(i):
            state = states[step, pl.ds(i * chunk, chunk)]
            near_features(nears[step % 2], rim + i * chunk, state)
            own_features(owns[step % 2], i * chunk, state)

    def build_halo(step):
        @pl.loop(0, rim // chunk)
        def _(i):
            near_features(nears[step % 2], i * chunk, halo_left[step, pl.ds(i * chunk, chunk)])
            near_features(nears[step % 2], rim + blocks + i * chunk, halo_right[step, pl.ds(i * chunk, chunk)])

    def pair_block(step):
        near, own = nears[step % 2], owns[step % 2]
        near_next, own_next = nears[(step + 1) % 2], owns[(step + 1) % 2]

        def one(block):
            fourth = tile_ref[step, 0, block] + tile_ref[step, 1, block] + tile_ref[step, 2, block]
            fourth = fourth + tile_ref[step, 3, block] - 3 * (block + rim)
            fourth = jnp.clip(fourth, 0, 2 * blocks - 1)
            mine = own[block]
            sums = jnp.zeros((16, LANES), F32)
            for pair in ((block, block + rim), (block + 2 * rim, fourth)):
                features = jnp.concatenate([near[pair[0]], near[pair[1]]], axis=1)
                weight = jnp.exp(dot(mine, features, 1, 0)).astype(BF16)
                sums = sums + dot(features[:16], weight, 1, 1)
            sums = sums[:8] + sums[8:]
            state = states[step, block]
            velocity = speed[step, block] + factor[block] * (state * sums[4:5] - sums)
            speed[step + 1, block] = velocity
            state = state + TIME_STEP * velocity
            states[step + 1, block] = state
            if step + 1 < OUTER * INNER:
                near_features(near_next, rim + block, state[None])
                own_features(own_next, block, state[None])

        return one

    def pair_rest(step, done):
        one = pair_block(step)
        left = blocks - done
        unroll = max(k for k in range(1, 9) if left % k == 0)

        @pl.loop(0, left // unroll)
        def _(i):
            for k in range(unroll):
                one(done + i * unroll + k)

    def beside(g, parts, part_body, each, step):
        one = pair_block(step)
        for k in range(max(parts, each)):
            if k < parts:
                part_body(k)
            if k < each:
                one(lax.rem(g * each + k, blocks))

    slot_index = solute_ref[...]
    pick_block = (lax.broadcasted_iota(jnp.int32, (blocks, slots), 0) == slot_index // LANES)
    pick_lane = (lax.broadcasted_iota(jnp.int32, (LANES, slots), 0) == slot_index % LANES)
    block_hot = pick_block.astype(F32)
    lane_hot = pick_lane.astype(F32)

    def gather_points(step, outer):
        found = []
        for axis in range(3):
            plane = states[step, :, axis, :].T
            parts = split3(plane)
            spread = sum(dot(part.astype(BF16), block_hot.astype(BF16), 1, 0) for part in parts)
            found.append(jnp.sum(spread * lane_hot, axis=0, keepdims=True))
        points[outer, me] = jnp.concatenate(
            found + [weight_ref[...], jnp.zeros((4, slots), F32)], axis=0
        )

    def amplitudes(outer, step, each):
        level[...] = jnp.zeros_like(level)
        width = slots

        @pl.loop(0, groups)
        def _(g):
            directions = table_ref[me, g]
            totals = [jnp.zeros((2 * e_half, 2 * f_half), F32)]

            def one_part(part):
                span = slice(part * width, (part + 1) * width)
                spot = points[outer, part]
                project = (
                    directions[:, 0:1] * spot[0:1] + directions[:, 1:2] * spot[1:2] + directions[:, 2:3] * spot[2:3]
                )

                def put(high_ref, low_ref, at, value):
                    high, low = split2(value)
                    high_ref[g, at : at + GROUP, span] = high
                    low_ref[g, at : at + GROUP, span] = low

                step_cos, step_sin = sincos(q_step * project)
                twice = 2.0 * step_cos
                old = (jnp.ones_like(project), jnp.zeros_like(project))
                new = (step_cos, step_sin)
                for b in range(fine):
                    put(f_high, f_low, b * GROUP, old[0])
                    put(f_high, f_low, f_half + b * GROUP, old[1])
                    old, new = new, (twice * new[0] - old[0], twice * new[1] - old[1])
                jump_cos, jump_sin = old
                if 3 * 2 * fine == coarse * fine:
                    real, imag = jump_cos * jump_cos - jump_sin * jump_sin, 2.0 * jump_cos * jump_sin
                else:
                    real, imag = sincos(project)
                scale = spot[3:4] * directions[:, 3:4]
                real, imag = real * scale, imag * scale
                for a in range(coarse):
                    put(e_high, e_low, a * GROUP, real)
                    put(e_high, e_low, e_half + a * GROUP, imag)
                    real, imag = real * jump_cos - imag * jump_sin, real * jump_sin + imag * jump_cos
                waves, bands = e_high[g, :, span], f_high[g, :, span]
                waves = jnp.concatenate([waves, waves, e_low[g, :, span]], axis=1)
                bands = jnp.concatenate([bands, f_low[g, :, span], bands], axis=1)
                totals[0] = totals[0] + dot(waves, bands, 1, 1)

            beside(g, count, one_part, each, step)
            total = totals[0]
            real = total[:e_half, :f_half] - total[e_half:, f_half:]
            imag = total[e_half:, :f_half] + total[:e_half, f_half:]
            amp_real[g] = real
            amp_imag[g] = imag
            level[...] += real * real + imag * imag

        diagonal = diagonal_mask()
        kept = jnp.where(diagonal, level[...], 0.0)
        sums = [jnp.sum(kept[a * GROUP : (a + 1) * GROUP], axis=0, keepdims=True) for a in range(coarse)]
        level_sp[outer, me] = jnp.concatenate(sums + [jnp.zeros((8 - coarse, f_half), F32)], axis=0)

    def diagonal_mask():
        rows = lax.broadcasted_iota(jnp.int32, (e_half, f_half), 0)
        columns = lax.broadcasted_iota(jnp.int32, (e_half, f_half), 1)
        return rows % GROUP == columns % GROUP

    def shell_gains(outer):
        total = level_rep[outer, 0]
        for k in range(1, replicas):
            total = total + level_rep[outer, k]
        rows = lax.broadcasted_iota(jnp.int32, (f_half, f_half), 0)
        columns = lax.broadcasted_iota(jnp.int32, (f_half, f_half), 1)
        same = (rows // GROUP == columns // GROUP).astype(F32)
        shells = dot(total, same, 1, 0, lax.Precision.HIGHEST) / (all_slots * M * replicas)
        count_shells = coarse * fine
        shell = lax.broadcasted_iota(jnp.int32, (8, count_shells), 1)
        in_row = shell // fine == lax.broadcasted_iota(jnp.int32, (8, count_shells), 0)
        shell = lax.broadcasted_iota(jnp.int32, (count_shells, f_half), 0)
        in_lane = shell % fine == lax.broadcasted_iota(jnp.int32, (count_shells, f_half), 1) // GROUP

        def spread(values):
            rows = jnp.where(in_row, values, 0.0)
            return dot(rows, in_lane.astype(F32), 1, 0, lax.Precision.HIGHEST)

        order = lax.broadcasted_iota(jnp.int32, (1, count_shells), 1).astype(F32)
        gain = precision_ref[...] * (1.0 + q_step * order) * (2.0 / (M * math.sqrt(all_slots)))
        coefficient = spread(gain) * (shells - spread(target_ref[...]))
        wide = jnp.concatenate(
            [jnp.broadcast_to(coefficient[a : a + 1], (GROUP, f_half)) for a in range(coarse)], axis=0
        )
        gains[...] = jnp.where(diagonal_mask(), wide, 0.0)

    def kicks(outer, step, each):
        kick_sum[...] = jnp.zeros_like(kick_sum)

        @pl.loop(0, groups)
        def _(g):
            real = gains[...] * amp_real[g]
            imag = gains[...] * amp_imag[g]
            mixed = jnp.concatenate(
                [jnp.concatenate([real, imag], axis=1), jnp.concatenate([imag, -real], axis=1)], axis=0
            )
            high, low = split2(mixed)
            mixed = jnp.concatenate([high, low, high], axis=1)
            directions = table_ref[me, g]
            def one_part(part):
                span = slice(part * slots, (part + 1) * slots)
                bands = f_high[g, :, span]
                turned = dot(mixed, jnp.concatenate([bands, bands, f_low[g, :, span]], axis=0), 1, 0)
                waves = e_high[g, :, span].astype(F32) + e_low[g, :, span].astype(F32)
                force = jnp.zeros((GROUP, slots), F32)
                for a in range(coarse):
                    here = slice(a * GROUP, (a + 1) * GROUP)
                    there = slice(e_half + a * GROUP, e_half + (a + 1) * GROUP)
                    force = force + waves[here] * turned[there] - waves[there] * turned[here]
                for axis in range(3):
                    kick_sum[axis, :, span] += directions[:, axis : axis + 1] * force

            beside(g, count, one_part, each, step)

        for part in range(count):
            span = slice(part * slots, (part + 1) * slots)
            sums = [-jnp.sum(kick_sum[axis, :, span], axis=0, keepdims=True) for axis in range(3)]
            kick_out[outer, part] = jnp.concatenate(sums + [jnp.zeros((5, slots), F32)], axis=0)

    def apply_kicks(outer, step):
        total = kick_in[outer, 0]
        for k in range(1, count):
            total = total + kick_in[outer, k]
        lanes = lane_hot.astype(BF16)
        for axis in range(3):
            parts = split3(total[axis : axis + 1] * block_hot)
            spread = sum(dot(part.astype(BF16), lanes, 1, 1) for part in parts)
            speed[step, :, axis, :] = speed[step, :, axis, :] + (INNER * TIME_STEP) * mass_ref[...] * spread

    start_halo(0)
    kick_copies = []
    for outer in range(OUTER):
        first = outer * INNER
        gather_points(first, outer)
        point_copies = group_copies(
            lambda d: points.at[outer, me], points.at[outer, me], point_send, point_recv, outer, sp_peer, count
        )
        start_all(point_copies)
        if outer == 0:
            build_own(first)
        else:
            wait_all(kick_copies)
            apply_kicks(outer - 1, first)
        finish_halo(first)
        build_halo(first)
        wait_all(point_copies)
        each = blocks // (groups + 3)
        amplitudes(outer, first, each)
        sp_copies = group_copies(
            lambda d: level_sp.at[outer, me], level_sp.at[outer, me], sp_send, sp_recv, outer, sp_peer, count
        )
        start_all(sp_copies)
        pair_rest(first, each * groups)
        start_halo(first + 1)
        wait_all(sp_copies)
        total = level_sp[outer, 0]
        for k in range(1, count):
            total = total + level_sp[outer, k]
        level_rep[outer, rep] = total
        rep_copies = group_copies(
            lambda d: level_rep.at[outer, rep], level_rep.at[outer, rep], rep_send, rep_recv, outer, rep_peer, replicas
        )
        start_all(rep_copies)
        finish_halo(first + 1)
        build_halo(first + 1)
        wait_all(rep_copies)
        shell_gains(outer)
        kicks(outer, first + 1, -(-blocks // groups))
        kick_in[outer, me] = kick_out[outer, me]
        kick_copies = group_copies(
            lambda d: kick_out.at[outer, lax.rem(me + d, count)],
            kick_in.at[outer, me],
            kick_send,
            kick_recv,
            outer,
            sp_peer,
            count,
        )
        start_all(kick_copies)
        for step in range(first + 2, first + INNER):
            start_halo(step)
            finish_halo(step)
            build_halo(step)
            pair_rest(step, 0)
        if outer + 1 < OUTER:
            start_halo(first + INNER)
    wait_all(kick_copies)
    apply_kicks(OUTER - 1, OUTER * INNER)
    for axis in range(3):
        pos_out[axis] = states[OUTER * INNER, :, axis, :]
        vel_out[axis] = speed[OUTER * INNER, :, axis, :]


def solution(mesh):
    count, replicas = mesh.shape["sp"], mesh.shape["rep"]
    table = direction_table(count)
    groups = table.shape[1]
    steps = OUTER * INNER

    def shards(
        positions, velocities, strength, inv_mass, tile_lists, solute_index, scatter_weight, intensity_exp, precision
    ):
        atoms = positions.shape[2]
        blocks = atoms // LANES
        rim = blocks // 2
        slots = solute_index.shape[1]
        shells = intensity_exp.shape[0]
        fine = LANES // GROUP
        coarse = shells // fine
        planes = (3, blocks, LANES)
        e_rows, f_rows, wide = 2 * coarse * GROUP, 2 * fine * GROUP, count * slots
        vmem = pl.BlockSpec(memory_space=pltpu.VMEM)
        dma = pltpu.SemaphoreType.DMA
        coords, speeds = pl.pallas_call(
            functools.partial(kernel, (count, replicas, blocks, slots, coarse, fine, groups)),
            out_shape=(
                jax.ShapeDtypeStruct(planes, F32),
                jax.ShapeDtypeStruct(planes, F32),
            ),
            in_specs=[pl.BlockSpec(memory_space=pltpu.SMEM)] + [vmem] * 9,
            out_specs=(vmem, vmem),
            scratch_shapes=[
                pltpu.VMEM((steps + 1, blocks, 8, LANES), F32),
                pltpu.VMEM((steps, rim, 8, LANES), F32),
                pltpu.VMEM((steps, rim, 8, LANES), F32),
                pltpu.VMEM((steps + 1, blocks, 8, LANES), F32),
                pltpu.VMEM((blocks, 8, LANES), F32),
                pltpu.VMEM((2 * blocks, ROWS, LANES), BF16),
                pltpu.VMEM((2 * blocks, ROWS, LANES), BF16),
                pltpu.VMEM((blocks, LANES, ROWS), BF16),
                pltpu.VMEM((blocks, LANES, ROWS), BF16),
                pltpu.VMEM((OUTER, count, 8, slots), F32),
                pltpu.VMEM((OUTER, count, 8, LANES), F32),
                pltpu.VMEM((OUTER, replicas, 8, LANES), F32),
                pltpu.VMEM((OUTER, count, 8, slots), F32),
                pltpu.VMEM((OUTER, count, 8, slots), F32),
                pltpu.VMEM((groups, e_rows, wide), BF16),
                pltpu.VMEM((groups, e_rows, wide), BF16),
                pltpu.VMEM((groups, f_rows, wide), BF16),
                pltpu.VMEM((groups, f_rows, wide), BF16),
                pltpu.VMEM((groups, e_rows // 2, f_rows // 2), F32),
                pltpu.VMEM((groups, e_rows // 2, f_rows // 2), F32),
                pltpu.VMEM((e_rows // 2, f_rows // 2), F32),
                pltpu.VMEM((e_rows // 2, f_rows // 2), F32),
                pltpu.VMEM((3, GROUP, wide), F32),
                dma((steps, 2)),
                dma((steps, 2)),
                dma((OUTER, count)),
                dma((OUTER, count)),
                dma((OUTER, count)),
                dma((OUTER, count)),
                dma((OUTER, replicas)),
                dma((OUTER, replicas)),
                dma((OUTER, count)),
                dma((OUTER, count)),
            ],
            compiler_params=pltpu.CompilerParams(
                collective_id=0, has_side_effects=True, vmem_limit_bytes=58 * 1024 * 1024
            ),
            cost_estimate=pl.CostEstimate(flops=40_000_000_000, bytes_accessed=4_000_000, transcendentals=20_000_000),
        )(
            jnp.transpose(tile_lists[0], (0, 2, 1)),
            positions.reshape(planes),
            velocities.reshape(planes),
            strength.reshape(blocks, LANES),
            inv_mass.reshape(blocks, LANES),
            solute_index,
            scatter_weight,
            intensity_exp.reshape(1, shells),
            precision.reshape(1, shells),
            jnp.asarray(table),
        )
        return coords.reshape(positions.shape), speeds.reshape(velocities.shape)

    in_specs = (
        P("rep", None, "sp"),
        P("rep", None, "sp"),
        P("rep", "sp"),
        P("rep", "sp"),
        P("rep", None, "sp", None),
        P("rep", "sp"),
        P("rep", "sp"),
        P(),
        P(),
    )
    out_specs = (P("rep", None, "sp"), P("rep", None, "sp"))
    return jax.shard_map(shards, mesh=mesh, in_specs=in_specs, out_specs=out_specs, check_vma=False)
```

```python
import functools
import math

import jax
import jax.numpy as jnp
import numpy as np
from jax import lax
from jax.experimental import pallas as pl
from jax.experimental.pallas import tpu as pltpu
from jax.sharding import PartitionSpec as P

M = 784
OUTER = 2
INNER = 2
TIME_STEP = 0.05
PAIR_STRENGTH = 0.2
HALF_INVERSE = 0.03125
LANES = 128
GROUP = 16
ROWS = 48
F32 = jnp.float32
BF16 = jnp.bfloat16
MESH = pl.DeviceIdType.MESH


def direction_table(shards):
    order = np.arange(M)
    height = 1.0 - (2.0 * order + 1.0) / M
    radius = np.sqrt(1.0 - height * height)
    azimuth = (order * 610 % 987) * (2.0 * math.pi / 987.0)
    rows = np.stack([radius * np.cos(azimuth), radius * np.sin(azimuth), height, np.ones(M)], axis=1)
    share = -(-M // shards)
    padded = -(-share // GROUP) * GROUP
    table = np.zeros((shards, padded, LANES), np.float32)
    for shard in range(shards):
        part = rows[shard * share : (shard + 1) * share]
        table[shard, : part.shape[0], :4] = part
    return table.reshape(shards, padded // GROUP, GROUP, LANES)


def dot(a, b, contract_a, contract_b, precision=None):
    return lax.dot_general(
        a, b, (((contract_a,), (contract_b,)), ((), ())), preferred_element_type=F32, precision=precision
    )


def split2(value):
    high = value.astype(BF16)
    return high, (value - high.astype(F32)).astype(BF16)


def split3(value):
    high = value.astype(BF16).astype(F32)
    rest = value - high
    middle = rest.astype(BF16).astype(F32)
    return high, middle, rest - middle


def sincos(angle):
    turns = jnp.floor(angle * (2.0 / math.pi) + 0.5)
    rest = angle - turns * 1.5703125
    rest = rest - turns * 4.837512969970703125e-4
    rest = rest - turns * 7.54978995489188216e-8
    square = rest * rest
    sine = rest + rest * square * (
        -1.6666654611e-1 + square * (8.3321608736e-3 - square * 1.9515295891e-4)
    )
    cosine = 1.0 - 0.5 * square + square * square * (
        4.166664568298827e-2 + square * (-1.388731625493765e-3 + square * 2.443315711809948e-5)
    )
    quadrant = turns.astype(jnp.int32)
    odd = (quadrant & 1) == 1
    first = jnp.where(odd, sine, cosine)
    second = jnp.where(odd, cosine, sine)
    first = jnp.where(((quadrant + 1) & 2) == 2, -first, first)
    second = jnp.where((quadrant & 2) == 2, -second, second)
    return first, second


def kernel(
    dims,
    tile_ref,
    pos_ref,
    vel_ref,
    strength_ref,
    mass_ref,
    solute_ref,
    weight_ref,
    target_ref,
    precision_ref,
    table_ref,
    pos_out,
    vel_out,
    states,
    halo_left,
    halo_right,
    speed,
    factor,
    near_even,
    near_odd,
    own_even,
    own_odd,
    points,
    level_sp,
    level_rep,
    kick_out,
    kick_in,
    e_high,
    e_low,
    f_high,
    f_low,
    amp_real,
    amp_imag,
    level,
    gains,
    kick_sum,
    halo_send,
    halo_recv,
    point_send,
    point_recv,
    sp_send,
    sp_recv,
    rep_send,
    rep_recv,
    kick_send,
    kick_recv,
):
    count, replicas, blocks, slots, coarse, fine, groups = dims
    rim = blocks // 2
    me = lax.axis_index("sp")
    rep = lax.axis_index("rep")
    q_step = 3.0 / (coarse * fine)
    all_slots = count * slots
    e_half = coarse * GROUP
    f_half = fine * GROUP

    def sp_peer(distance):
        return (rep, lax.rem(me + distance, count))

    def rep_peer(distance):
        return (lax.rem(rep + distance, replicas), me)

    barrier = pltpu.get_barrier_semaphore()
    for distance in range(1, count):
        pl.semaphore_signal(barrier, inc=1, device_id=sp_peer(distance), device_id_type=MESH)
    for distance in range(1, replicas):
        pl.semaphore_signal(barrier, inc=1, device_id=rep_peer(distance), device_id_type=MESH)

    row = lax.broadcasted_iota(jnp.int32, (1, 8, LANES), 1)
    strength = strength_ref[...]
    push = (TIME_STEP * PAIR_STRENGTH / math.sqrt(4 * LANES)) * strength * mass_ref[...]
    states[0] = jnp.broadcast_to(jnp.where(row == 4, 1.0, 0.0), (blocks, 8, LANES))
    speed[...] = jnp.zeros_like(speed)
    factor[...] = jnp.zeros_like(factor)
    states[0, :, 3, :] = jnp.log(strength)
    for axis in range(3):
        states[0, :, axis, :] = pos_ref[axis]
        speed[:, axis, :] = vel_ref[axis]
        factor[:, axis, :] = push

    @pl.when(me == 0)
    def _():
        halo_left[...] = jnp.zeros_like(halo_left)

    @pl.when(me == count - 1)
    def _():
        halo_right[...] = jnp.zeros_like(halo_right)

    pl.semaphore_wait(barrier, count - 1 + replicas - 1)

    def halo_copies(step):
        to_right = pltpu.make_async_remote_copy(
            src_ref=states.at[step, pl.ds(blocks - rim, rim)],
            dst_ref=halo_left.at[step],
            send_sem=halo_send.at[step, 0],
            recv_sem=halo_recv.at[step, 0],
            device_id=sp_peer(1),
            device_id_type=MESH,
        )
        to_left = pltpu.make_async_remote_copy(
            src_ref=states.at[step, pl.ds(0, rim)],
            dst_ref=halo_right.at[step],
            send_sem=halo_send.at[step, 1],
            recv_sem=halo_recv.at[step, 1],
            device_id=sp_peer(count - 1),
            device_id_type=MESH,
        )
        return to_right, to_left

    def start_halo(step):
        to_right, to_left = halo_copies(step)
        pl.when(me < count - 1)(to_right.start)
        pl.when(me > 0)(to_left.start)

    def finish_halo(step):
        to_right, to_left = halo_copies(step)
        pl.when(me < count - 1)(to_right.wait_send)
        pl.when(me > 0)(to_left.wait_send)
        pl.when(me > 0)(to_right.wait_recv)
        pl.when(me < count - 1)(to_left.wait_recv)

    def group_copies(source, target, send, recv, outer, peer, size):
        return [
            pltpu.make_async_remote_copy(
                src_ref=source(distance),
                dst_ref=target,
                send_sem=send.at[outer, distance],
                recv_sem=recv.at[outer, distance],
                device_id=peer(distance),
                device_id_type=MESH,
            )
            for distance in range(1, size)
        ]

    def start_all(copies):
        for copy in copies:
            copy.start()

    def wait_all(copies):
        for copy in copies:
            copy.wait()

    def block_features(state):
        radius = HALF_INVERSE * jnp.sum(jnp.where(row < 3, state * state, 0.0), axis=1, keepdims=True)
        return radius, jnp.where(row == 3, state - radius, state)

    def near_features(near, target, state):
        radius, value = block_features(state)
        high, middle, low = split3(value)
        near[pl.ds(target, state.shape[0])] = jnp.concatenate(
            [high, middle, high, middle, low, high], axis=1
        ).astype(BF16)

    def own_features(own, index, state):
        radius, value = block_features(state)
        near_side = jnp.where(row < 3, state * (2.0 * HALF_INVERSE), 0.0)
        value = near_side + jnp.where(row == 3, 1.0, 0.0) - jnp.where(row == 4, radius, 0.0)
        high, middle, low = split3(value)
        rows = jnp.concatenate([high, high, middle, middle, high, low], axis=1)
        for k in range(state.shape[0]):
            own[index + k] = rows[k].T.astype(BF16)

    chunk = 8
    nears, owns = (near_even, near_odd), (own_even, own_odd)

    def build_own(step):
        @pl.loop(0, blocks // chunk)
        def _(i):
            state = states[step, pl.ds(i * chunk, chunk)]
            near_features(nears[step % 2], rim + i * chunk, state)
            own_features(owns[step % 2], i * chunk, state)

    def build_halo(step):
        @pl.loop(0, rim // chunk)
        def _(i):
            near_features(nears[step % 2], i * chunk, halo_left[step, pl.ds(i * chunk, chunk)])
            near_features(nears[step % 2], rim + blocks + i * chunk, halo_right[step, pl.ds(i * chunk, chunk)])

    def pair_step(step):
        near, own = nears[step % 2], owns[step % 2]
        near_next, own_next = nears[(step + 1) % 2], owns[(step + 1) % 2]

        unroll = 8 if blocks % 8 == 0 else 1

        @pl.loop(0, blocks // unroll)
        def _(i):
            start = i * unroll
            sides = []
            for k in range(unroll):
                block = start + k
                fourth = tile_ref[step, 0, block] + tile_ref[step, 1, block] + tile_ref[step, 2, block]
                fourth = fourth + tile_ref[step, 3, block] - 3 * (block + rim)
                fourth = jnp.clip(fourth, 0, 2 * blocks - 1)
                sides.append(((block, block + rim), (block + 2 * rim, fourth)))

            def weigh(k):
                mine = own[start + k]
                found = []
                for pair in sides[k]:
                    features = jnp.concatenate([near[pair[0]], near[pair[1]]], axis=1)
                    found.append((features[:16], jnp.exp(dot(mine, features, 1, 0)).astype(BF16)))
                return found

            def add_up(found):
                sums = jnp.zeros((16, LANES), F32)
                for features, weight in found:
                    sums = sums + dot(features, weight, 1, 1)
                return sums[:8] + sums[8:]

            sums, held = [], weigh(0)
            for k in range(1, unroll):
                ahead = weigh(k)
                sums.append(add_up(held))
                held = ahead
            sums.append(add_up(held))
            sums = jnp.stack(sums)
            here = pl.ds(start, unroll)
            state = states[step, here]
            velocity = speed[here] + factor[here] * (state * sums[:, 4:5] - sums)
            speed[here] = velocity
            state = state + TIME_STEP * velocity
            states[step + 1, here] = state
            if step + 1 < OUTER * INNER:
                near_features(near_next, rim + start, state)
                own_features(own_next, start, state)

    slot_index = solute_ref[...]
    pick_block = (lax.broadcasted_iota(jnp.int32, (blocks, slots), 0) == slot_index // LANES)
    pick_lane = (lax.broadcasted_iota(jnp.int32, (LANES, slots), 0) == slot_index % LANES)
    block_hot = pick_block.astype(F32)
    lane_hot = pick_lane.astype(F32)

    def gather_points(step, outer):
        found = []
        for axis in range(3):
            plane = states[step, :, axis, :].T
            parts = split3(plane)
            spread = sum(dot(part.astype(BF16), block_hot.astype(BF16), 1, 0) for part in parts)
            found.append(jnp.sum(spread * lane_hot, axis=0, keepdims=True))
        points[outer, me] = jnp.concatenate(
            found + [weight_ref[...], jnp.zeros((4, slots), F32)], axis=0
        )

    def amplitudes(outer):
        level[...] = jnp.zeros_like(level)
        width = slots

        @pl.loop(0, groups)
        def _(g):
            directions = table_ref[me, g]
            total = jnp.zeros((2 * e_half, 2 * f_half), F32)
            for part in range(count):
                span = slice(part * width, (part + 1) * width)
                spot = points[outer, part]
                project = (
                    directions[:, 0:1] * spot[0:1] + directions[:, 1:2] * spot[1:2] + directions[:, 2:3] * spot[2:3]
                )

                def put(high_ref, low_ref, at, value):
                    high, low = split2(value)
                    high_ref[g, at : at + GROUP, span] = high
                    low_ref[g, at : at + GROUP, span] = low

                step_cos, step_sin = sincos(q_step * project)
                twice = 2.0 * step_cos
                old = (jnp.ones_like(project), jnp.zeros_like(project))
                new = (step_cos, step_sin)
                for b in range(fine):
                    put(f_high, f_low, b * GROUP, old[0])
                    put(f_high, f_low, f_half + b * GROUP, old[1])
                    old, new = new, (twice * new[0] - old[0], twice * new[1] - old[1])
                jump_cos, jump_sin = old
                if 3 * 2 * fine == coarse * fine:
                    real, imag = jump_cos * jump_cos - jump_sin * jump_sin, 2.0 * jump_cos * jump_sin
                else:
                    real, imag = sincos(project)
                scale = spot[3:4] * directions[:, 3:4]
                real, imag = real * scale, imag * scale
                for a in range(coarse):
                    put(e_high, e_low, a * GROUP, real)
                    put(e_high, e_low, e_half + a * GROUP, imag)
                    real, imag = real * jump_cos - imag * jump_sin, real * jump_sin + imag * jump_cos
                waves, bands = e_high[g, :, span], f_high[g, :, span]
                waves = jnp.concatenate([waves, waves, e_low[g, :, span]], axis=1)
                bands = jnp.concatenate([bands, f_low[g, :, span], bands], axis=1)
                total = total + dot(waves, bands, 1, 1)
            real = total[:e_half, :f_half] - total[e_half:, f_half:]
            imag = total[e_half:, :f_half] + total[:e_half, f_half:]
            amp_real[g] = real
            amp_imag[g] = imag
            level[...] += real * real + imag * imag

        diagonal = diagonal_mask()
        kept = jnp.where(diagonal, level[...], 0.0)
        sums = [jnp.sum(kept[a * GROUP : (a + 1) * GROUP], axis=0, keepdims=True) for a in range(coarse)]
        level_sp[outer, me] = jnp.concatenate(sums + [jnp.zeros((8 - coarse, f_half), F32)], axis=0)

    def diagonal_mask():
        rows = lax.broadcasted_iota(jnp.int32, (e_half, f_half), 0)
        columns = lax.broadcasted_iota(jnp.int32, (e_half, f_half), 1)
        return rows % GROUP == columns % GROUP

    def shell_gains(outer):
        total = level_rep[outer, 0]
        for k in range(1, replicas):
            total = total + level_rep[outer, k]
        rows = lax.broadcasted_iota(jnp.int32, (f_half, f_half), 0)
        columns = lax.broadcasted_iota(jnp.int32, (f_half, f_half), 1)
        same = (rows // GROUP == columns // GROUP).astype(F32)
        shells = dot(total, same, 1, 0, lax.Precision.HIGHEST) / (all_slots * M * replicas)
        count_shells = coarse * fine
        shell = lax.broadcasted_iota(jnp.int32, (8, count_shells), 1)
        in_row = shell // fine == lax.broadcasted_iota(jnp.int32, (8, count_shells), 0)
        shell = lax.broadcasted_iota(jnp.int32, (count_shells, f_half), 0)
        in_lane = shell % fine == lax.broadcasted_iota(jnp.int32, (count_shells, f_half), 1) // GROUP

        def spread(values):
            rows = jnp.where(in_row, values, 0.0)
            return dot(rows, in_lane.astype(F32), 1, 0, lax.Precision.HIGHEST)

        order = lax.broadcasted_iota(jnp.int32, (1, count_shells), 1).astype(F32)
        gain = precision_ref[...] * (1.0 + q_step * order) * (2.0 / (M * math.sqrt(all_slots)))
        coefficient = spread(gain) * (shells - spread(target_ref[...]))
        wide = jnp.concatenate(
            [jnp.broadcast_to(coefficient[a : a + 1], (GROUP, f_half)) for a in range(coarse)], axis=0
        )
        gains[...] = jnp.where(diagonal_mask(), wide, 0.0)

    def kicks(outer):
        kick_sum[...] = jnp.zeros_like(kick_sum)

        @pl.loop(0, groups)
        def _(g):
            real = gains[...] * amp_real[g]
            imag = gains[...] * amp_imag[g]
            mixed = jnp.concatenate(
                [jnp.concatenate([real, imag], axis=1), jnp.concatenate([imag, -real], axis=1)], axis=0
            )
            high, low = split2(mixed)
            mixed = jnp.concatenate([high, low, high], axis=1)
            directions = table_ref[me, g]
            for part in range(count):
                span = slice(part * slots, (part + 1) * slots)
                bands = f_high[g, :, span]
                turned = dot(mixed, jnp.concatenate([bands, bands, f_low[g, :, span]], axis=0), 1, 0)
                waves = e_high[g, :, span].astype(F32) + e_low[g, :, span].astype(F32)
                force = jnp.zeros((GROUP, slots), F32)
                for a in range(coarse):
                    here = slice(a * GROUP, (a + 1) * GROUP)
                    there = slice(e_half + a * GROUP, e_half + (a + 1) * GROUP)
                    force = force + waves[here] * turned[there] - waves[there] * turned[here]
                for axis in range(3):
                    kick_sum[axis, :, span] += directions[:, axis : axis + 1] * force

        for part in range(count):
            span = slice(part * slots, (part + 1) * slots)
            sums = [-jnp.sum(kick_sum[axis, :, span], axis=0, keepdims=True) for axis in range(3)]
            kick_out[outer, part] = jnp.concatenate(sums + [jnp.zeros((5, slots), F32)], axis=0)

    def apply_kicks(outer):
        total = kick_in[outer, 0]
        for k in range(1, count):
            total = total + kick_in[outer, k]
        lanes = lane_hot.astype(BF16)
        for axis in range(3):
            parts = split3(total[axis : axis + 1] * block_hot)
            spread = sum(dot(part.astype(BF16), lanes, 1, 1) for part in parts)
            speed[:, axis, :] = speed[:, axis, :] + (INNER * TIME_STEP) * mass_ref[...] * spread

    start_halo(0)
    kick_copies = []
    for outer in range(OUTER):
        first = outer * INNER
        gather_points(first, outer)
        point_copies = group_copies(
            lambda d: points.at[outer, me], points.at[outer, me], point_send, point_recv, outer, sp_peer, count
        )
        start_all(point_copies)
        if outer == 0:
            build_own(first)
        else:
            wait_all(kick_copies)
            apply_kicks(outer - 1)
            finish_halo(first)
            build_halo(first)
        wait_all(point_copies)
        amplitudes(outer)
        sp_copies = group_copies(
            lambda d: level_sp.at[outer, me], level_sp.at[outer, me], sp_send, sp_recv, outer, sp_peer, count
        )
        start_all(sp_copies)
        if outer == 0:
            finish_halo(first)
            build_halo(first)
        wait_all(sp_copies)
        total = level_sp[outer, 0]
        for k in range(1, count):
            total = total + level_sp[outer, k]
        level_rep[outer, rep] = total
        rep_copies = group_copies(
            lambda d: level_rep.at[outer, rep], level_rep.at[outer, rep], rep_send, rep_recv, outer, rep_peer, replicas
        )
        start_all(rep_copies)
        pair_step(first)
        for inner in range(1, INNER):
            step = first + inner
            start_halo(step)
            if inner == 1:
                wait_all(rep_copies)
                shell_gains(outer)
                kicks(outer)
                kick_in[outer, me] = kick_out[outer, me]
                kick_copies = group_copies(
                    lambda d: kick_out.at[outer, lax.rem(me + d, count)],
                    kick_in.at[outer, me],
                    kick_send,
                    kick_recv,
                    outer,
                    sp_peer,
                    count,
                )
                start_all(kick_copies)
            finish_halo(step)
            build_halo(step)
            pair_step(step)
        if outer + 1 < OUTER:
            start_halo(first + INNER)
    wait_all(kick_copies)
    apply_kicks(OUTER - 1)
    for axis in range(3):
        pos_out[axis] = states[OUTER * INNER, :, axis, :]
        vel_out[axis] = speed[:, axis, :]


def solution(mesh):
    count, replicas = mesh.shape["sp"], mesh.shape["rep"]
    table = direction_table(count)
    groups = table.shape[1]
    steps = OUTER * INNER

    def shards(
        positions, velocities, strength, inv_mass, tile_lists, solute_index, scatter_weight, intensity_exp, precision
    ):
        atoms = positions.shape[2]
        blocks = atoms // LANES
        rim = blocks // 2
        slots = solute_index.shape[1]
        shells = intensity_exp.shape[0]
        fine = LANES // GROUP
        coarse = shells // fine
        planes = (3, blocks, LANES)
        e_rows, f_rows, wide = 2 * coarse * GROUP, 2 * fine * GROUP, count * slots
        vmem = pl.BlockSpec(memory_space=pltpu.VMEM)
        dma = pltpu.SemaphoreType.DMA
        coords, speeds = pl.pallas_call(
            functools.partial(kernel, (count, replicas, blocks, slots, coarse, fine, groups)),
            out_shape=(
                jax.ShapeDtypeStruct(planes, F32),
                jax.ShapeDtypeStruct(planes, F32),
            ),
            in_specs=[pl.BlockSpec(memory_space=pltpu.SMEM)] + [vmem] * 9,
            out_specs=(vmem, vmem),
            scratch_shapes=[
                pltpu.VMEM((steps + 1, blocks, 8, LANES), F32),
                pltpu.VMEM((steps, rim, 8, LANES), F32),
                pltpu.VMEM((steps, rim, 8, LANES), F32),
                pltpu.VMEM((blocks, 8, LANES), F32),
                pltpu.VMEM((blocks, 8, LANES), F32),
                pltpu.VMEM((2 * blocks, ROWS, LANES), BF16),
                pltpu.VMEM((2 * blocks, ROWS, LANES), BF16),
                pltpu.VMEM((blocks, LANES, ROWS), BF16),
                pltpu.VMEM((blocks, LANES, ROWS), BF16),
                pltpu.VMEM((OUTER, count, 8, slots), F32),
                pltpu.VMEM((OUTER, count, 8, LANES), F32),
                pltpu.VMEM((OUTER, replicas, 8, LANES), F32),
                pltpu.VMEM((OUTER, count, 8, slots), F32),
                pltpu.VMEM((OUTER, count, 8, slots), F32),
                pltpu.VMEM((groups, e_rows, wide), BF16),
                pltpu.VMEM((groups, e_rows, wide), BF16),
                pltpu.VMEM((groups, f_rows, wide), BF16),
                pltpu.VMEM((groups, f_rows, wide), BF16),
                pltpu.VMEM((groups, e_rows // 2, f_rows // 2), F32),
                pltpu.VMEM((groups, e_rows // 2, f_rows // 2), F32),
                pltpu.VMEM((e_rows // 2, f_rows // 2), F32),
                pltpu.VMEM((e_rows // 2, f_rows // 2), F32),
                pltpu.VMEM((3, GROUP, wide), F32),
                dma((steps, 2)),
                dma((steps, 2)),
                dma((OUTER, count)),
                dma((OUTER, count)),
                dma((OUTER, count)),
                dma((OUTER, count)),
                dma((OUTER, replicas)),
                dma((OUTER, replicas)),
                dma((OUTER, count)),
                dma((OUTER, count)),
            ],
            compiler_params=pltpu.CompilerParams(
                collective_id=0, has_side_effects=True, vmem_limit_bytes=58 * 1024 * 1024
            ),
            cost_estimate=pl.CostEstimate(flops=40_000_000_000, bytes_accessed=4_000_000, transcendentals=20_000_000),
        )(
            jnp.transpose(tile_lists[0], (0, 2, 1)),
            positions.reshape(planes),
            velocities.reshape(planes),
            strength.reshape(blocks, LANES),
            inv_mass.reshape(blocks, LANES),
            solute_index,
            scatter_weight,
            intensity_exp.reshape(1, shells),
            precision.reshape(1, shells),
            jnp.asarray(table),
        )
        return coords.reshape(positions.shape), speeds.reshape(velocities.shape)

    in_specs = (
        P("rep", None, "sp"),
        P("rep", None, "sp"),
        P("rep", "sp"),
        P("rep", "sp"),
        P("rep", None, "sp", None),
        P("rep", "sp"),
        P("rep", "sp"),
        P(),
        P(),
    )
    out_specs = (P("rep", None, "sp"), P("rep", None, "sp"))
    return jax.shard_map(shards, mesh=mesh, in_specs=in_specs, out_specs=out_specs, check_vma=False)
```
